32 devices in a mesh: ctx: 16 (over z, x, core), head: 2 (over y).
Axes of the slice: x: 2, y: 2, z: 4, core: 2. Of those that a mesh axis runs over, the one named last changes fastest.
Arguments:
- query: bfloat16 [2048, 4096], P('ctx', 'head'), may hold values from -12 to 12
- key: bfloat16 [2048, 1024], P('ctx', 'head'), may hold values from -6 to 6
- value: bfloat16 [2048, 1024], P('ctx', 'head'), may hold values from -6 to 6
- held_kv: bfloat16 [2, 2048, 1024], P(None, 'ctx', 'head'), may hold values from -6 to 6
- plan: int32 [16, 4], replicated, may hold values from 0 to 15
Outputs:
- attended: bfloat16 [2048, 4096], P(('ctx', 'head'))
- log_total: float32 [32, 2048], P('head', 'ctx')
The draws below stay inside these ranges and needn't reach their ends.
All inputs are finite; a program needn't handle non-finite values.
Results may differ from the reference program's by a relative error of at most 0.012.
Values may be sent and summed in bfloat16 or wider, within the bound.
No kernel may reach another device: no remote copies, remote signals or barrier semaphores. Data moves between devices by JAX's collectives and lax.ppermute only.
A program may use at most 64 MiB of HBM per device.

```python
import math
import jax
import jax.numpy as jnp
from jax import lax

QH = 32
KVH = 8
HD = 128
TOK_DEV = 128
QB = 4
STEPS = 3
KS = 6
SUB = 32
TOKENS = 2048
ENTRIES = 16
N_CTX = 16


def draw_query(key, part):
    group = QH // KVH
    result = jnp.clip(2.0 * jax.random.normal(jax.random.fold_in(key, 11), (TOKENS, KVH, group, HD)), -12.0, 12.0)
    return result.astype(jnp.float32).reshape(TOKENS, QH * HD).astype(jnp.bfloat16)


def draw_key(key, part):
    result = jnp.clip(jax.random.normal(jax.random.fold_in(key, 13), (TOKENS, KVH, HD)), -6.0, 6.0)
    return result.astype(jnp.float32).reshape(TOKENS, KVH * HD).astype(jnp.bfloat16)


def draw_plan(key, part):
    half_count = ENTRIES // (STEPS - 1)
    helper_ids = jnp.arange(half_count, dtype=jnp.int32)
    dropped = jax.random.randint(jax.random.fold_in(key, 3), (half_count,), 0, STEPS, dtype=jnp.int32)
    dropped = jnp.where(helper_ids == half_count - 1, 0, dropped)
    offsets = jnp.arange(1, STEPS, dtype=jnp.int32)
    steps_all = ((dropped[:, None] + offsets[None, :]) % STEPS).reshape(-1)
    helpers = jnp.repeat(helper_ids, STEPS - 1)
    owners = helpers + half_count
    blocks = jax.random.randint(jax.random.fold_in(key, 5), (ENTRIES,), 0, QB, dtype=jnp.int32)
    return jnp.stack([steps_all, helpers, owners, blocks], axis=1).astype(jnp.int32)


def levels(key, shape, cuts, low, top_value):
    loudness, own = 1.0, jax.random.fold_in(key, 6)
    for position, parts in cuts:
        draws = jnp.exp(jax.random.uniform(jax.random.fold_in(own, position), (parts,), jnp.float32, low / len(cuts), top_value / len(cuts)))
        loudness = loudness * jnp.repeat(draws, shape[position] // parts).reshape([-1 if axis == position else 1 for axis in range(len(shape))])
    return loudness


def scatter_about(key, shape, scale, bound, cuts=(), held_as=jnp.bfloat16):
    loudness = levels(key, shape, cuts, -0.22, 0.18) if cuts else 1.0
    values = jax.random.normal(key, shape, jnp.float32) * scale * loudness
    return jnp.minimum(jnp.maximum(values, -bound), bound).astype(held_as)


def setup_inputs(seed: int = 0) -> dict:
    streams_of = jax.random.split(jax.random.key(seed), 6)
    return {
        "query": draw_query(jax.random.fold_in(streams_of[5], 71), 0),
        "key": draw_key(jax.random.fold_in(streams_of[5], 71), 0),
        "value": scatter_about(streams_of[2], (TOKENS, KVH * HD), 1.0, 6.0, ((0, 16), (1, 2))),
        "held_kv": scatter_about(streams_of[3], (2, TOKENS, KVH * HD), 1.0, 6.0, ((1, 16), (2, 2))),
        "plan": draw_plan(jax.random.fold_in(streams_of[5], 71), 0),
    }


def reference(query, key, value, held_kv, plan):
    group = QH // KVH
    score_scale = 1.0 / math.sqrt(HD)
    sched_step = plan[:, 0]
    sched_helper = plan[:, 1]
    sched_owner = plan[:, 2]
    sched_block = plan[:, 3]
    positions = jnp.arange(TOK_DEV, dtype=jnp.int32)
    causal = positions[:, None] >= positions[None, :]
    sub_index = positions // SUB

    def rows_of(source, block_id):
        start = (block_id * TOK_DEV).astype(jnp.int32)
        return lax.dynamic_slice_in_dim(source, start, TOK_DEV, 0).reshape(TOK_DEV, KVH, HD)

    def one_block(block_id):
        key_list = [rows_of(key, block_id)]
        value_list = [rows_of(value, block_id)]
        mask_list = [causal]
        for cycle_step in range(STEPS):
            regular_ok = block_id >= KS + cycle_step
            source_id = jnp.maximum(block_id - cycle_step, 0).astype(jnp.int32)
            key_list.append(rows_of(held_kv[0], source_id))
            value_list.append(rows_of(held_kv[1], source_id))
            mask_list.append(jnp.broadcast_to(regular_ok, (TOK_DEV, TOK_DEV)))
        for cycle_step in range(STEPS):
            match = (sched_step == cycle_step) & (sched_owner == block_id)
            found = jnp.any(match)
            helper_id = jnp.sum(jnp.where(match, sched_helper, 0))
            chosen = jnp.sum(jnp.where(match, sched_block, 0))
            source_id = ((helper_id - cycle_step) % N_CTX).astype(jnp.int32)
            key_list.append(rows_of(held_kv[0], source_id))
            value_list.append(rows_of(held_kv[1], source_id))
            row_ok = found & (sub_index == chosen)
            mask_list.append(jnp.broadcast_to(row_ok[:, None], (TOK_DEV, TOK_DEV)))
        key_all = jnp.concatenate(key_list, axis=0).astype(jnp.float32)
        value_all = jnp.concatenate(value_list, axis=0).astype(jnp.float32)
        seen = jnp.concatenate(mask_list, axis=1)
        start = (block_id * TOK_DEV).astype(jnp.int32)
        query_rows = lax.dynamic_slice_in_dim(query, start, TOK_DEV, 0).reshape(TOK_DEV, KVH, group, HD)
        scores = jnp.einsum('rkhd,skd->khrs', query_rows.astype(jnp.float32), key_all) * score_scale
        scores = jnp.where(seen, scores, -jnp.inf)
        highest = lax.optimization_barrier(jnp.max(scores, axis=-1, keepdims=True))
        log_total = highest[..., 0] + jnp.log(lax.optimization_barrier(jnp.sum(jnp.exp(scores - highest), axis=-1)))
        weights = jnp.exp(scores - log_total[..., None]).astype(jnp.bfloat16)
        weights = lax.optimization_barrier(weights)
        mixed = jnp.einsum('khrs,skd->rkhd', weights.astype(jnp.float32), value_all)
        return (mixed.astype(jnp.bfloat16).reshape(TOK_DEV, QH * HD), log_total.reshape(QH, TOK_DEV))
    outputs, totals = lax.map(one_block, jnp.arange(N_CTX, dtype=jnp.int32))
    attended = outputs.reshape(TOKENS, QH * HD)
    log_total = jnp.transpose(totals, (1, 0, 2)).reshape(QH, TOKENS)
    return (attended, log_total)
```

```python
import functools
import math

import jax
import jax.numpy as jnp
from jax import lax
from jax.experimental import pallas as pl
from jax.experimental.pallas import tpu as pltpu
from jax.sharding import PartitionSpec as P

HD = 128
QB = 4
STEPS = 3
CHUNKS = ((0, 2), (2, 2))
SCALE = 1.0 / math.sqrt(HD)
LOG2E = math.log2(math.e)
NEG = -math.inf

SMEM = pl.BlockSpec(memory_space=pltpu.SMEM)
VMEM = pl.BlockSpec(memory_space=pltpu.VMEM)
ANY = pl.BlockSpec(memory_space=pl.ANY)


def stacked(q_ref, kv_head, group):
    first = kv_head * group
    return jnp.concatenate(
        [q_ref[:, (first + j) * HD : (first + j + 1) * HD] for j in range(group)], axis=0
    )


def scores_of(keys, queries):
    return lax.dot_general(
        keys, queries, (((1,), (1,)), ((), ())), preferred_element_type=jnp.float32
    )


def mix(values, weights):
    return lax.dot_general(
        values,
        weights.astype(jnp.bfloat16),
        (((0,), (0,)), ((), ())),
        preferred_element_type=jnp.float32,
    )


def local_kernel(half, entries, idx_ref, plan_ref, q_ref, k_ref, v_ref, held_ref, acc_ref, stat_ref, meta_ref):
    rows = q_ref.shape[0]
    kv_heads = k_ref.shape[1] // HD
    group = q_ref.shape[1] // k_ref.shape[1]
    device = idx_ref[0]
    for t in range(STEPS):
        meta_ref[t] = -1

    def scan(i, carry):
        @pl.when(plan_ref[i, 2] == device)
        def _():
            meta_ref[plan_ref[i, 0]] = plan_ref[i, 3]

        return carry

    lax.fori_loop(0, entries, scan, 0)
    held_bias = jnp.where(device >= half - 2, 0.0, NEG)
    key_pos = lax.broadcasted_iota(jnp.int32, (rows, group * rows), 0)
    row_pos = lax.broadcasted_iota(jnp.int32, (rows, group * rows), 1) % rows
    causal = key_pos <= row_pos
    for g in range(kv_heads):
        cols = slice(g * HD, (g + 1) * HD)
        queries = stacked(q_ref, g, group)
        own = jnp.where(causal, scores_of(k_ref[:, cols], queries), NEG)
        held = scores_of(held_ref[0, :, cols], queries) + held_bias
        top = jnp.maximum(
            jnp.max(own, axis=0, keepdims=True), jnp.max(held, axis=0, keepdims=True)
        )
        w_own = jnp.exp2((own - top) * (SCALE * LOG2E))
        w_held = jnp.exp2((held - top) * (SCALE * LOG2E))
        stat_ref[g, 0:1, :] = top
        stat_ref[g, 1:2, :] = jnp.sum(w_own, axis=0, keepdims=True) + jnp.sum(
            w_held, axis=0, keepdims=True
        )
        acc_ref[g] = mix(v_ref[:, cols], w_own) + mix(held_ref[1, :, cols], w_held)


def final_kernel(
    half, first, count,
    idx_ref, meta_ref, q_ref, acc_ref, stat_ref,
    n2, sx, sn2, w, sw, f, h, sf, sh,
    mine_ref, send_ref, log_ref,
    kv, sem,
):
    rows = q_ref.shape[0]
    group = q_ref.shape[1] // (count * HD)
    device = idx_ref[0]
    head = idx_ref[1]
    even = device % 2 == 0
    wide = pl.ds(first * HD, count * HD)
    step_a = jnp.where(meta_ref[0] >= 0, 0, 1)
    step_b = jnp.where(meta_ref[2] >= 0, 2, 1)

    def pick(slot, source, when, whole):
        @pl.when(when)
        def _():
            part = source.at[:, :, wide] if whole else source
            pltpu.make_async_copy(part, kv.at[slot], sem.at[slot]).start()

    pick(0, sn2, even, True)
    pick(0, sx, jnp.logical_not(even), True)
    pick(1, n2, device >= 0, True)
    for slot, step in ((2, step_a), (3, step_b)):
        if slot == 2:
            pick(slot, f, step == 0, False)
        else:
            pick(slot, w, (step == 2) & (device <= half + 1), True)
            pick(slot, h, (step == 2) & (device > half + 1), False)
        pick(slot, sf, (step == 1) & jnp.logical_not(even), False)
        pick(slot, sw, (step == 1) & even & (device <= half), True)
        pick(slot, sh, (step == 1) & even & (device > half), False)
    for slot in range(4):
        pltpu.make_async_copy(f, kv.at[slot], sem.at[slot]).wait()

    lane = lax.broadcasted_iota(jnp.int32, (1, group * rows), 1)
    sub = (lane % rows) // (rows // QB)
    biases = [
        jnp.where(device >= half - 1, 0.0, NEG),
        jnp.where(device >= half, 0.0, NEG),
        jnp.where(sub == meta_ref[step_a], 0.0, NEG),
        jnp.where(sub == meta_ref[step_b], 0.0, NEG),
    ]
    for g in range(count):
        cols = slice(g * HD, (g + 1) * HD)
        queries = stacked(q_ref, g, group)
        scores = [scores_of(kv[s, 0, :, cols], queries) + biases[s] for s in range(4)]
        old_top = stat_ref[g, 0:1, :]
        top = old_top
        for s in scores:
            top = jnp.maximum(top, jnp.max(s, axis=0, keepdims=True))
        keep = jnp.exp2((old_top - top) * (SCALE * LOG2E))
        total = stat_ref[g, 1:2, :] * keep
        mixed = acc_ref[g] * keep
        for slot, s in enumerate(scores):
            weights = jnp.exp2((s - top) * (SCALE * LOG2E))
            total = total + jnp.sum(weights, axis=0, keepdims=True)
            mixed = mixed + mix(kv[slot, 1, :, cols], weights)
        mixed = mixed * (1.0 / total)
        logs = top * SCALE + jnp.log(total)
        for j in range(group):
            out = jnp.transpose(mixed[:, j * rows : (j + 1) * rows]).astype(jnp.bfloat16)
            low, high = out[: rows // 2], out[rows // 2 :]
            at = slice((g * group + j) * HD, (g * group + j + 1) * HD)
            mine_ref[:, at] = jnp.where(head == 0, low, high)
            send_ref[:, at] = jnp.where(head == 0, high, low)
            log_ref[g * group + j : g * group + j + 1, :] = logs[:, j * rows : (j + 1) * rows]


def shards(query, key, value, held_kv, plan):
    rows = query.shape[0]
    kv_heads = key.shape[1] // HD
    group = query.shape[1] // key.shape[1]
    size = lax.axis_size("ctx")
    half = size // 2
    device = lax.axis_index("ctx")
    head = lax.axis_index("head")
    idx = jnp.stack([device, head]).astype(jnp.int32)

    def send(x, route):
        return lax.ppermute(x, "ctx", route)

    owners = range(half, size)
    n2 = send(held_kv, [(b - 2, b) for b in owners])
    sx = send(held_kv, [(b, b + 1) for b in range(half - 2, size, 2)])
    w = send(held_kv, [(size - 2, half), (size - 1, half + 1)])
    sw = send(w, [(half + 1, half)])
    sn2 = send(n2, [(b + 1, b) for b in range(half, size, 2)])

    acc, stat, meta = pl.pallas_call(
        functools.partial(local_kernel, half, plan.shape[0]),
        out_shape=(
            jax.ShapeDtypeStruct((kv_heads, HD, group * rows), jnp.float32),
            jax.ShapeDtypeStruct((kv_heads, 2, group * rows), jnp.float32),
            jax.ShapeDtypeStruct((STEPS,), jnp.int32),
        ),
        in_specs=[SMEM, SMEM, VMEM, VMEM, VMEM, VMEM],
        out_specs=(VMEM, VMEM, SMEM),
        name="local",
    )(idx, plan, query, key, value, held_kv)

    pieces = []
    for first, count in CHUNKS:
        part = held_kv[:, :, first * HD : (first + count) * HD]
        f = send(part, [(b - half, b) for b in range(half, size - 1)])
        h = send(f, [(b - 2, b) for b in range(half + 2, size)])
        sf = send(f, [(b, b + 1) for b in range(half, size, 2)])
        sh = send(h, [(b + 1, b) for b in range(half + 2, size, 2)])
        wide = count * group * HD
        at = first // count
        mine, away, logs = pl.pallas_call(
            functools.partial(final_kernel, half, first, count),
            grid=(1,),
            out_shape=(
                jax.ShapeDtypeStruct((rows // 2, wide), jnp.bfloat16),
                jax.ShapeDtypeStruct((rows // 2, wide), jnp.bfloat16),
                jax.ShapeDtypeStruct((count * group, rows), jnp.float32),
            ),
            in_specs=[
                SMEM,
                SMEM,
                pl.BlockSpec((rows, wide), lambda i, at=at: (0, at)),
                pl.BlockSpec((count, HD, group * rows), lambda i, at=at: (at, 0, 0)),
                pl.BlockSpec((count, 2, group * rows), lambda i, at=at: (at, 0, 0)),
            ]
            + [ANY] * 9,
            out_specs=(
                pl.BlockSpec((rows // 2, wide), lambda i: (0, 0)),
                pl.BlockSpec((rows // 2, wide), lambda i: (0, 0)),
                pl.BlockSpec((count * group, rows), lambda i: (0, 0)),
            ),
            scratch_shapes=[
                pltpu.VMEM((4, 2, rows, count * HD), jnp.bfloat16),
                pltpu.SemaphoreType.DMA((4,)),
            ],
            name="final",
        )(idx, meta, query, acc, stat, n2, sx, sn2, w, sw, f, h, sf, sh)
        there = lax.ppermute(away, "head", [(0, 1), (1, 0)])
        pieces.append((mine, there, logs))
    mine = jnp.concatenate([p[0] for p in pieces], axis=1)
    there = jnp.concatenate([p[1] for p in pieces], axis=1)
    attended = jnp.where(
        head == 0,
        jnp.concatenate([mine, there], axis=1),
        jnp.concatenate([there, mine], axis=1),
    )
    return (attended, jnp.concatenate([p[2] for p in pieces], axis=0))


def solution(mesh):
    return jax.shard_map(
        shards,
        mesh=mesh,
        in_specs=(
            P("ctx", "head"),
            P("ctx", "head"),
            P("ctx", "head"),
            P(None, "ctx", "head"),
            P(),
        ),
        out_specs=(P(("ctx", "head"), None), P("head", "ctx")),
        check_vma=False,
    )
```

```python
import functools
import math

import jax
import jax.numpy as jnp
from jax import lax
from jax.experimental import pallas as pl
from jax.experimental.pallas import tpu as pltpu
from jax.sharding import PartitionSpec as P

HD = 128
QB = 4
STEPS = 3
CHUNKS = ((0, 4),)
SCALE = 1.0 / math.sqrt(HD)
LN2 = math.log(2.0)
FACTOR = SCALE / LN2
NEG = -math.inf

SMEM = pl.BlockSpec(memory_space=pltpu.SMEM)
VMEM = pl.BlockSpec(memory_space=pltpu.VMEM)
PARAMS = pltpu.CompilerParams(vmem_limit_bytes=16 * 2**20)
COST = pl.CostEstimate(flops=1000, bytes_accessed=1000, transcendentals=0)
ANY = pl.BlockSpec(memory_space=pl.ANY)


def stacked(q_ref, kv_head, group):
    first = kv_head * group
    return jnp.concatenate(
        [q_ref[:, (first + j) * HD : (first + j + 1) * HD] for j in range(group)], axis=0
    )


def scores_of(keys, queries):
    return lax.dot_general(
        keys, queries, (((1,), (1,)), ((), ())), preferred_element_type=jnp.float32
    )


def mix(values, weights):
    return lax.dot_general(
        values,
        weights,
        (((0,), (0,)), ((), ())),
        preferred_element_type=jnp.float32,
    )


def local_kernel(half, entries, idx_ref, plan_ref, q_ref, k_ref, v_ref, held_ref, acc_ref, stat_ref, meta_ref):
    rows = q_ref.shape[0]
    kv_heads = k_ref.shape[1] // HD
    group = q_ref.shape[1] // k_ref.shape[1]
    device = idx_ref[0]
    for t in range(STEPS):
        meta_ref[t] = -1

    def scan(i, carry):
        @pl.when(plan_ref[i, 2] == device)
        def _():
            meta_ref[plan_ref[i, 0]] = plan_ref[i, 3]

        return carry

    lax.fori_loop(0, entries, scan, 0)
    held_bias = jnp.where(device >= half - 2, 0.0, NEG)
    key_pos = lax.broadcasted_iota(jnp.int32, (rows, group * rows), 0)
    row_pos = lax.broadcasted_iota(jnp.int32, (rows, group * rows), 1) % rows
    causal = key_pos <= row_pos
    for g in range(kv_heads):
        cols = slice(g * HD, (g + 1) * HD)
        queries = stacked(q_ref, g, group)
        own = jnp.where(causal, scores_of(k_ref[:, cols], queries), NEG)
        held = scores_of(held_ref[0, :, cols], queries) + held_bias
        top = jnp.maximum(
            jnp.max(own, axis=0, keepdims=True), jnp.max(held, axis=0, keepdims=True)
        )
        w_own = jnp.exp2((own - top) * FACTOR)
        w_held = jnp.exp2((held - top) * FACTOR)
        stat_ref[g, 0:1, :] = top
        stat_ref[g, 1:2, :] = jnp.sum(w_own, axis=0, keepdims=True) + jnp.sum(
            w_held, axis=0, keepdims=True
        )
        acc_ref[g] = mix(v_ref[:, cols], w_own.astype(jnp.bfloat16)) + mix(
            held_ref[1, :, cols], w_held.astype(jnp.bfloat16)
        )


def near_kernel(
    half, first, count,
    idx_ref, q_ref, acc_ref, stat_ref,
    n2, sx, sn2, f, sf,
    base_ref, log_ref, sub_ref,
    kv,
):
    rows = q_ref.shape[0]
    group = QB
    device = idx_ref[0]
    even = device % 2 == 0
    odd = jnp.logical_not(even)
    corner = device <= half + 1
    inner = jnp.logical_not(corner)
    pick = functools.partial(bring, kv, first, count)
    pick(0, sx, odd, True)
    pick(0, sf, even & corner, False)
    pick(0, sn2, even & inner, True)
    pick(1, f, corner, False)
    pick(1, n2, inner, True)
    first_key = lax.broadcasted_iota(jnp.int32, (2 * rows, 1), 0) < rows
    bias = jnp.where(
        first_key,
        jnp.where(device >= half - 1, 0.0, NEG),
        jnp.where(device >= half, 0.0, NEG),
    )
    sub = rows // QB
    for g in range(count):
        cols = slice(g * HD, (g + 1) * HD)
        queries = stacked(q_ref, first + g, group)
        scores = scores_of(kv[0, :, cols], queries) + bias
        old_top = stat_ref[first + g, 0:1, :]
        top = jnp.maximum(old_top, jnp.max(scores, axis=0, keepdims=True))
        keep = jnp.exp2((old_top - top) * FACTOR)
        weights = jnp.exp2((scores - top) * FACTOR)
        total = stat_ref[first + g, 1:2, :] * keep + jnp.sum(weights, axis=0, keepdims=True)
        inverse = 1.0 / total
        mixed = acc_ref[first + g] * (keep * inverse) + mix(
            kv[1, :, cols], (weights * inverse).astype(jnp.bfloat16)
        )
        logs = top * FACTOR + jnp.log2(total)
        for j in range(group):
            lanes = slice(j * rows, (j + 1) * rows)
            at = slice((g * group + j) * HD, (g * group + j + 1) * HD)
            base_ref[:, at] = jnp.transpose(mixed[:, lanes]).astype(jnp.bfloat16)
            log_ref[g * group + j : g * group + j + 1, :] = logs[:, lanes]
        for c in range(QB):
            part = [logs[:, j * rows + c * sub : j * rows + (c + 1) * sub] for j in range(group)]
            sub_ref[c * count + g : c * count + g + 1, :] = jnp.concatenate(part, axis=1)


def bring(kv, first, count, slot, source, when, whole):
    @pl.when(when)
    def _():
        rows = source.shape[1]
        at = slice(slot * rows, (slot + 1) * rows)
        if whole:
            kv[:, at, :] = source[:, :, first * HD : (first + count) * HD]
        else:
            kv[:, at, :] = source[...]


def far_kernel(
    half, first, count,
    idx_ref, meta_ref, q_ref, base_ref, sub_ref,
    n2, sn2, f, h, sf, sh,
    mine_ref, send_ref, new_ref,
    kv,
):
    rows = q_ref.shape[0]
    sub = rows // QB
    group = QB
    device = idx_ref[0]
    head = idx_ref[1]
    step_a = jnp.where(meta_ref[0] >= 0, 0, 1)
    step_b = jnp.where(meta_ref[2] >= 0, 2, 1)
    owner = device >= half

    @pl.when(owner)
    def _():
        even = device % 2 == 0
        odd = jnp.logical_not(even)
        corner = device <= half + 1
        inner = jnp.logical_not(corner)
        pick = functools.partial(bring, kv, first, count)
        pick(0, h, step_a == 0, False)
        pick(1, n2, (step_b == 2) & corner, True)
        pick(1, f, (step_b == 2) & inner, False)
        for slot, step in ((0, step_a), (1, step_b)):
            pick(slot, sh, (step == 1) & odd, False)
            pick(slot, sn2, (step == 1) & even & corner, True)
            pick(slot, sf, (step == 1) & even & inner, False)

    def half_rows(which):
        return pl.ds(pl.multiple_of(which * (rows // 2), rows // 2), rows // 2)

    mine_ref[...] = base_ref[half_rows(head), :]
    send_ref[...] = base_ref[half_rows(1 - head), :]

    @pl.when(owner)
    def _():
        chosen = [meta_ref[step_a], meta_ref[step_b]]
        at_rows = [pl.ds(pl.multiple_of(c * sub, sub), sub) for c in chosen]
        lanes = group * sub
        first_key = lax.broadcasted_iota(jnp.int32, (2 * rows, 2 * lanes), 0) < rows
        first_row = lax.broadcasted_iota(jnp.int32, (2 * rows, 2 * lanes), 1) < lanes
        bias = jnp.where(first_key == first_row, 0.0, jnp.where(chosen[0] == chosen[1], 0.0, NEG))
        results = []
        for g in range(count):
            cols = slice(g * HD, (g + 1) * HD)
            names = range(g * group, (g + 1) * group)

            def rows_of(ref, skip):
                parts = [ref[at, (skip + j) * HD : (skip + j + 1) * HD] for at in at_rows for j in names]
                return jnp.concatenate(parts, axis=0)

            scores = scores_of(kv[0, :, cols], rows_of(q_ref, first * group)) * FACTOR + bias
            old_log = jnp.concatenate([sub_ref[pl.ds(c * count + g, 1), :] for c in chosen], axis=1)
            top = jnp.maximum(old_log, jnp.max(scores, axis=0, keepdims=True))
            weights = jnp.exp2(scores - top)
            keep = jnp.exp2(old_log - top)
            total = keep + jnp.sum(weights, axis=0, keepdims=True)
            inverse = 1.0 / total
            share = jnp.transpose(jnp.broadcast_to(keep * inverse, (8, 2 * lanes)))[:, 0:1]
            final = mix((weights * inverse).astype(jnp.bfloat16), kv[1, :, cols]) + rows_of(base_ref, 0).astype(jnp.float32) * share
            new_log = top + jnp.log2(total)
            for slot in range(2):
                new_ref[slot * count + g : slot * count + g + 1, :] = new_log[:, slot * lanes : (slot + 1) * lanes]
                part = final[slot * lanes : (slot + 1) * lanes].astype(jnp.bfloat16)
                results.append((chosen[slot], names, part))
        for chosen, names, final in results:
            at_half = pl.ds(pl.multiple_of(chosen % (QB // 2) * sub, sub), sub)
            for target, here in ((mine_ref, True), (send_ref, False)):

                @pl.when((chosen // (QB // 2) == head) == here)
                def _():
                    for i, j in enumerate(names):
                        target[at_half, j * HD : (j + 1) * HD] = final[i * sub : (i + 1) * sub]


def log_kernel(chunks, meta_ref, *refs):
    n = len(chunks)
    logs, news, log_ref = refs[:n], refs[n : 2 * n], refs[2 * n]
    rows = log_ref.shape[1]
    sub = rows // QB
    step_a = jnp.where(meta_ref[0] >= 0, 0, 1)
    step_b = jnp.where(meta_ref[2] >= 0, 2, 1)
    row_sub = lax.broadcasted_iota(jnp.int32, (1, rows), 1) // sub
    for log, new, (first, count) in zip(logs, news, chunks):
        heads = log.shape[0]
        group = heads // count
        for j in range(heads):
            result = log[j : j + 1, :]
            for slot, step in ((0, step_a), (1, step_b)):
                chosen = meta_ref[step]
                at = slot * count + j // group
                moved = pltpu.roll(new[at : at + 1, :], (chosen + QB - j % group) % QB * sub, 1)
                result = jnp.where(row_sub == chosen, moved, result)
            log_ref[first * group + j : first * group + j + 1, :] = result * LN2


def shards(query, key, value, held_kv, plan):
    rows = query.shape[0]
    kv_heads = key.shape[1] // HD
    group = query.shape[1] // key.shape[1]
    size = lax.axis_size("ctx")
    half = size // 2
    device = lax.axis_index("ctx")
    head = lax.axis_index("head")
    idx = jnp.stack([device, head]).astype(jnp.int32)

    def send(x, route):
        return lax.ppermute(x, "ctx", route)

    swap = [(i, i ^ 1) for i in range(size)]
    onward = swap[:half] + [(i, half + (i - half + 2) % half) for i in range(half, size)]
    back = [(j, i) for i, j in onward]
    across = [(i, half + (i + 2) % half) for i in range(half)]
    across += [(j, i) for i, j in across]

    parts = [held_kv[:, :, a * HD : (a + n) * HD] for a, n in CHUNKS]
    n2 = send(held_kv, onward)
    sx = send(held_kv, swap)
    fs = [send(part, across) for part in parts]

    acc, stat, meta = pl.pallas_call(
        functools.partial(local_kernel, half, plan.shape[0]),
        out_shape=(
            jax.ShapeDtypeStruct((kv_heads, HD, group * rows), jnp.float32),
            jax.ShapeDtypeStruct((kv_heads, 2, group * rows), jnp.float32),
            jax.ShapeDtypeStruct((STEPS,), jnp.int32),
        ),
        in_specs=[SMEM, SMEM, VMEM, VMEM, VMEM, VMEM],
        out_specs=(VMEM, VMEM, SMEM),
        compiler_params=PARAMS,
        cost_estimate=COST,
        name="local",
    )(idx, plan, query, key, value, held_kv)

    fs, n2, acc, stat, meta = lax.optimization_barrier((fs, n2, acc, stat, meta))
    sn2 = send(n2, swap)

    def near(first, count, f, sf):
        wide = count * group * HD
        return pl.pallas_call(
            functools.partial(near_kernel, half, first, count),
            out_shape=(
                jax.ShapeDtypeStruct((rows, wide), jnp.bfloat16),
                jax.ShapeDtypeStruct((count * group, rows), jnp.float32),
                jax.ShapeDtypeStruct((QB * count, rows // QB * group), jnp.float32),
            ),
            in_specs=[SMEM] + [VMEM] * 8,
            out_specs=(VMEM,) * 3,
            scratch_shapes=[pltpu.VMEM((2, 2 * rows, count * HD), jnp.bfloat16)],
            compiler_params=PARAMS,
            cost_estimate=COST,
            name="near",
        )(idx, query, acc, stat, n2, sx, sn2, f, sf)

    def far(first, count, base, subs, f, h, sf, sh):
        wide = count * group * HD
        return pl.pallas_call(
            functools.partial(far_kernel, half, first, count),
            out_shape=(
                jax.ShapeDtypeStruct((rows // 2, wide), jnp.bfloat16),
                jax.ShapeDtypeStruct((rows // 2, wide), jnp.bfloat16),
                jax.ShapeDtypeStruct((2 * count, rows // QB * group), jnp.float32),
            ),
            in_specs=[SMEM, SMEM] + [VMEM] * 9,
            out_specs=(VMEM,) * 3,
            scratch_shapes=[pltpu.VMEM((2, 2 * rows, count * HD), jnp.bfloat16)],
            compiler_params=PARAMS,
            cost_estimate=COST,
            name="far",
        )(idx, meta, query, base, subs, n2, sn2, f, h, sf, sh)

    n = len(CHUNKS)
    sfs = [send(f, swap) for f in fs]
    hs, near_parts = [], []
    for k, (f, sf) in enumerate(zip(fs, sfs)):
        if k > 0:
            f, held_back = lax.optimization_barrier((f, near_parts[-1][0]))
            near_parts[-1] = (held_back, *near_parts[-1][1:])
        hs.append(send(f, back))
        near_parts.append(near(*CHUNKS[k], f, sf))
    hs[0], near_parts = lax.optimization_barrier((hs[0], near_parts))
    mine, news, there = [], [], []
    for k, (base, log, table) in enumerate(near_parts):
        h = hs[k]
        if k > 0:
            h, away = lax.optimization_barrier((h, away))
            there.append(lax.ppermute(away, "head", [(0, 1), (1, 0)]))
        sh = send(h, swap)
        piece, away, new = far(*CHUNKS[k], base, table, fs[k], h, sfs[k], sh)
        mine.append(piece)
        news.append(new)
    there.append(lax.ppermute(away, "head", [(0, 1), (1, 0)]))
    logs = [log for _, log, _ in near_parts]
    log_total = pl.pallas_call(
        functools.partial(log_kernel, CHUNKS),
        out_shape=jax.ShapeDtypeStruct((kv_heads * group, rows), jnp.float32),
        in_specs=[SMEM] + [VMEM] * (2 * n),
        out_specs=VMEM,
        compiler_params=PARAMS,
        cost_estimate=COST,
        name="logs",
    )(meta, *logs, *news)
    mine, there = jnp.concatenate(mine, axis=1), jnp.concatenate(there, axis=1)
    attended = jnp.where(
        head == 0,
        jnp.concatenate([mine, there], axis=1),
        jnp.concatenate([there, mine], axis=1),
    )
    return (attended, log_total)


def solution(mesh):
    return jax.shard_map(
        shards,
        mesh=mesh,
        in_specs=(
            P("ctx", "head"),
            P("ctx", "head"),
            P("ctx", "head"),
            P(None, "ctx", "head"),
            P(),
        ),
        out_specs=(P(("ctx", "head"), None), P("head", "ctx")),
        check_vma=False,
    )
```

```python
import functools
import math

import jax
import jax.numpy as jnp
from jax import lax
from jax.experimental import pallas as pl
from jax.experimental.pallas import tpu as pltpu
from jax.sharding import PartitionSpec as P

HD = 128
QB = 4
STEPS = 3
LN2 = math.log(2.0)
FACTOR = 1.0 / (math.sqrt(HD) * LN2)
NEG = -math.inf

SMEM = pl.BlockSpec(memory_space=pltpu.SMEM)
VMEM = pl.BlockSpec(memory_space=pltpu.VMEM)
PARAMS = pltpu.CompilerParams(vmem_limit_bytes=16 * 2**20)
COST = pl.CostEstimate(flops=1000, bytes_accessed=1000, transcendentals=0)


def stacked(q_ref, kv_head, group):
    first = kv_head * group
    return jnp.concatenate([q_ref[:, (first + j) * HD : (first + j + 1) * HD] for j in range(group)], axis=0)


def scores_of(keys, queries):
    return lax.dot_general(keys, queries, (((1,), (1,)), ((), ())), preferred_element_type=jnp.float32)


def mix(left, right):
    return lax.dot_general(left, right, (((0,), (0,)), ((), ())), preferred_element_type=jnp.float32)


def local_kernel(half, entries, idx_ref, plan_ref, q_ref, k_ref, v_ref, held_ref, acc_ref, stat_ref, meta_ref):
    rows = q_ref.shape[0]
    kv_heads = k_ref.shape[1] // HD
    group = q_ref.shape[1] // k_ref.shape[1]
    device = idx_ref[0]
    for t in range(STEPS):
        meta_ref[t] = -1

    def scan(i, carry):
        @pl.when(plan_ref[i, 2] == device)
        def _():
            meta_ref[plan_ref[i, 0]] = plan_ref[i, 3]

        return carry

    lax.fori_loop(0, entries, scan, 0)
    held_bias = jnp.where(device >= half - 2, 0.0, NEG)
    key_pos = lax.broadcasted_iota(jnp.int32, (rows, group * rows), 0)
    row_pos = lax.broadcasted_iota(jnp.int32, (rows, group * rows), 1) % rows
    causal = key_pos <= row_pos
    for g in range(kv_heads):
        cols = slice(g * HD, (g + 1) * HD)
        queries = stacked(q_ref, g, group)
        own = jnp.where(causal, scores_of(k_ref[:, cols], queries), NEG)
        held = scores_of(held_ref[0, :, cols], queries) + held_bias
        top = jnp.maximum(jnp.max(own, axis=0, keepdims=True), jnp.max(held, axis=0, keepdims=True))
        w_own = jnp.exp2((own - top) * FACTOR)
        w_held = jnp.exp2((held - top) * FACTOR)
        stat_ref[g, 0:1, :] = top
        stat_ref[g, 1:2, :] = jnp.sum(w_own, axis=0, keepdims=True) + jnp.sum(w_held, axis=0, keepdims=True)
        acc_ref[g] = mix(v_ref[:, cols], w_own.astype(jnp.bfloat16)) + mix(
            held_ref[1, :, cols], w_held.astype(jnp.bfloat16)
        )


def near_kernel(half, idx_ref, q_ref, acc_ref, stat_ref, n2, sx, sn2, base_ref, log_ref, sub_ref, kv):
    rows = q_ref.shape[0]
    kv_heads = n2.shape[2] // HD
    group = q_ref.shape[1] // n2.shape[2]
    sub = rows // QB
    device = idx_ref[0]
    even = device % 2 == 0

    @pl.when(even)
    def _():
        kv[:, :rows, :] = sn2[...]

    @pl.when(jnp.logical_not(even))
    def _():
        kv[:, :rows, :] = sx[...]

    kv[:, rows:, :] = n2[...]
    first_key = lax.broadcasted_iota(jnp.int32, (2 * rows, 1), 0) < rows
    bias = jnp.where(
        first_key,
        jnp.where(device >= half - 1, 0.0, NEG),
        jnp.where(device >= half, 0.0, NEG),
    )
    for g in range(kv_heads):
        cols = slice(g * HD, (g + 1) * HD)
        scores = scores_of(kv[0, :, cols], stacked(q_ref, g, group)) + bias
        old_top = stat_ref[g, 0:1, :]
        top = jnp.maximum(old_top, jnp.max(scores, axis=0, keepdims=True))
        keep = jnp.exp2((old_top - top) * FACTOR)
        weights = jnp.exp2((scores - top) * FACTOR)
        total = stat_ref[g, 1:2, :] * keep + jnp.sum(weights, axis=0, keepdims=True)
        inverse = 1.0 / total
        mixed = acc_ref[g] * (keep * inverse) + mix(kv[1, :, cols], (weights * inverse).astype(jnp.bfloat16))
        logs = top * FACTOR + jnp.log2(total)
        for j in range(group):
            lanes = slice(j * rows, (j + 1) * rows)
            at = g * group + j
            base_ref[:, at * HD : (at + 1) * HD] = jnp.transpose(mixed[:, lanes]).astype(jnp.bfloat16)
            log_ref[at : at + 1, :] = logs[:, lanes]
        for c in range(QB):
            part = [logs[:, j * rows + c * sub : j * rows + (c + 1) * sub] for j in range(group)]
            sub_ref[c * kv_heads + g : c * kv_heads + g + 1, :] = jnp.concatenate(part, axis=1)


def helped(device, meta_ref):
    even = device % 2 == 0
    return meta_ref[1], jnp.where(even, meta_ref[0], meta_ref[2]), jnp.where(even, meta_ref[2], meta_ref[0])


def update(old_log, old, keys, values, queries, bias):
    scores = scores_of(keys, queries) * FACTOR
    if bias is not None:
        scores = scores + bias
    top = jnp.maximum(old_log, jnp.max(scores, axis=0, keepdims=True))
    weights = jnp.exp2(scores - top)
    keep = jnp.exp2(old_log - top)
    total = keep + jnp.sum(weights, axis=0, keepdims=True)
    inverse = 1.0 / total
    share = jnp.transpose(jnp.broadcast_to(keep * inverse, (8, keep.shape[1])))[:, 0:1]
    mixed = mix((weights * inverse).astype(jnp.bfloat16), values) + old.astype(jnp.float32) * share
    return mixed.astype(jnp.bfloat16), top + jnp.log2(total)


def rows_of(ref, starts, names):
    sub = ref.shape[0] // QB
    parts = [ref[pl.ds(pl.multiple_of(c * sub, sub), sub), j * HD : (j + 1) * HD] for c in starts for j in names]
    return jnp.concatenate(parts, axis=0)


def early_kernel(
    half, idx_ref, meta_ref, q_ref, base_ref, sub_ref, f, sf, g1, sg, full_ref, mine_ref, send_ref, new_ref, kv
):
    rows = q_ref.shape[0]
    sub = rows // QB
    kv_heads = f.shape[2] // HD
    group = q_ref.shape[1] // f.shape[2]
    device = idx_ref[0]
    head = idx_ref[1]
    full_ref[...] = base_ref[...]

    @pl.when(device >= half)
    def _():
        last = device == 2 * half - 1

        @pl.when(last)
        def _():
            kv[:, :rows, :] = g1[...]

        @pl.when(jnp.logical_not(last))
        def _():
            kv[:, :rows, :] = f[...]

        @pl.when(device == 2 * half - 2)
        def _():
            kv[:, rows:, :] = sg[...]

        @pl.when(device != 2 * half - 2)
        def _():
            kv[:, rows:, :] = sf[...]

        chosen = helped(device, meta_ref)[:2]
        starts = [jnp.maximum(c, 0) for c in chosen]
        lanes = group * sub
        first_key = lax.broadcasted_iota(jnp.int32, (2 * rows, 2 * lanes), 0) < rows
        first_row = lax.broadcasted_iota(jnp.int32, (2 * rows, 2 * lanes), 1) < lanes
        bias = jnp.where(first_key == first_row, 0.0, jnp.where(chosen[0] == chosen[1], 0.0, NEG))
        results = []
        for g in range(kv_heads):
            cols = slice(g * HD, (g + 1) * HD)
            names = range(g * group, (g + 1) * group)
            final, log = update(
                jnp.concatenate([sub_ref[pl.ds(c * kv_heads + g, 1), :] for c in starts], axis=1),
                rows_of(base_ref, starts, names),
                kv[0, :, cols],
                kv[1, :, cols],
                rows_of(q_ref, starts, names),
                bias,
            )
            for slot in range(2):
                part = slice(slot * lanes, (slot + 1) * lanes)
                new_ref[slot * kv_heads + g : slot * kv_heads + g + 1, :] = log[:, part]
                results.append((slot, names, final[part]))
        for slot in range(2):

            @pl.when(chosen[slot] >= 0)
            def _():
                at_rows = pl.ds(pl.multiple_of(starts[slot] * sub, sub), sub)
                for which, names, final in results:
                    if which == slot:
                        for i, j in enumerate(names):
                            full_ref[at_rows, j * HD : (j + 1) * HD] = final[i * sub : (i + 1) * sub]

    half_rows = rows // 2
    mine_ref[...] = full_ref[pl.ds(pl.multiple_of(head * half_rows, half_rows), half_rows), :]
    send_ref[...] = full_ref[pl.ds(pl.multiple_of((1 - head) * half_rows, half_rows), half_rows), :]


def late_kernel(half, idx_ref, meta_ref, q_ref, full_ref, sub_ref, new_ref, h, late_ref, log_ref):
    rows = q_ref.shape[0]
    sub = rows // QB
    kv_heads = h.shape[2] // HD
    group = q_ref.shape[1] // h.shape[2]
    device = idx_ref[0]
    first, second, chosen = helped(device, meta_ref)

    @pl.when(chosen >= 0)
    def _():
        for g in range(kv_heads):
            cols = slice(g * HD, (g + 1) * HD)
            names = range(g * group, (g + 1) * group)
            old_log = sub_ref[pl.ds(chosen * kv_heads + g, 1), :]
            old_log = jnp.where(first == chosen, new_ref[g : g + 1, :], old_log)
            old_log = jnp.where(second == chosen, new_ref[kv_heads + g : kv_heads + g + 1, :], old_log)
            final, log = update(
                old_log,
                rows_of(full_ref, [chosen], names),
                h[0, :, cols],
                h[1, :, cols],
                rows_of(q_ref, [chosen], names),
                None,
            )
            log_ref[g : g + 1, :] = log
            for i, j in enumerate(names):
                late_ref[:, j * HD : (j + 1) * HD] = final[i * sub : (i + 1) * sub]


def log_kernel(idx_ref, meta_ref, old_ref, new_ref, late_ref, log_ref):
    heads, rows = log_ref.shape
    kv_heads = late_ref.shape[0]
    group = heads // kv_heads
    sub = rows // QB
    row_sub = lax.broadcasted_iota(jnp.int32, (1, rows), 1) // sub
    first, second, third = helped(idx_ref[0], meta_ref)
    for j in range(heads):
        result = old_ref[j : j + 1, :]
        for chosen, source, at in (
            (first, new_ref, j // group),
            (second, new_ref, kv_heads + j // group),
            (third, late_ref, j // group),
        ):
            moved = pltpu.roll(source[at : at + 1, :], (chosen + QB - j % group) % QB * sub, 1)
            result = jnp.where(row_sub == chosen, moved, result)
        log_ref[j : j + 1, :] = result * LN2


def call(kernel, name, outs, scratch, *args, scalars):
    return pl.pallas_call(
        kernel,
        out_shape=outs,
        in_specs=[SMEM] * scalars + [VMEM] * (len(args) - scalars),
        out_specs=[SMEM if out.shape == (STEPS,) else VMEM for out in outs],
        scratch_shapes=scratch,
        compiler_params=PARAMS,
        cost_estimate=COST,
        name=name,
    )(*args)


def shards(query, key, value, held_kv, plan):
    rows = query.shape[0]
    sub = rows // QB
    wide = query.shape[1]
    kv_heads = key.shape[1] // HD
    group = wide // key.shape[1]
    size = lax.axis_size("ctx")
    half = size // 2
    device = lax.axis_index("ctx")
    head = lax.axis_index("head")
    idx = jnp.stack([device, head]).astype(jnp.int32)

    def send(x, route):
        return lax.ppermute(x, "ctx", route)

    def other_head(x):
        return lax.ppermute(x, "head", [(0, 1), (1, 0)])

    def f32(*shape):
        return jax.ShapeDtypeStruct(shape, jnp.float32)

    def b16(*shape):
        return jax.ShapeDtypeStruct(shape, jnp.bfloat16)

    swap = [(i, i ^ 1) for i in range(size)]
    two_on = swap[: half - 2] + [(i, i + 2) for i in range(half - 2, size - 2)]
    two_on += [(i, i - half) for i in range(size - 2, size)]
    across = [(i, i + half + 1) for i in range(half - 2)] + swap[half - 2 : half]
    across += [(i, i - half) for i in range(half, size - 2)] + [(size - 2, size - 1), (size - 1, half)]
    extra = [(half - 2, size - 1), (size - 1, size - 2), (size - 2, half - 1), (half - 1, half - 2)]
    moved = {i for i, _ in extra}
    extra += [(i, j) for i, j in swap if i not in moved]
    beside = swap[:half] + [(i, half + (i - half + (1 if i % 2 else -1)) % half) for i in range(half, size)]

    n2 = send(held_kv, two_on)
    sx = send(held_kv, swap)
    f = send(held_kv, across)
    acc, stat, meta = call(
        functools.partial(local_kernel, half, plan.shape[0]),
        "local",
        (f32(kv_heads, HD, group * rows), f32(kv_heads, 2, group * rows), jax.ShapeDtypeStruct((STEPS,), jnp.int32)),
        (),
        idx, plan, query, key, value, held_kv,
        scalars=2,
    )
    held_late, acc = lax.optimization_barrier((held_kv, acc))
    g1 = send(held_late, extra)
    pair = pltpu.VMEM((2, 2 * rows, key.shape[1]), jnp.bfloat16)
    outs = (b16(rows, wide), f32(kv_heads * group, rows), f32(QB * kv_heads, group * sub))

    def near(n2, sx, acc, stat):
        sn2 = send(n2, swap)
        return tuple(
            call(functools.partial(near_kernel, half), "near", outs, (pair,), idx, query, acc, stat, n2, sx, sn2, scalars=1)
        )

    def none(n2, sx, acc, stat):
        return tuple(jnp.zeros(out.shape, out.dtype) for out in outs)

    base, logs, table = lax.cond(plan[0, 0] >= 0, near, none, n2, sx, acc, stat)
    f, base = lax.optimization_barrier((f, base))
    h = send(f, beside)
    sf = send(f, swap)
    sg = send(g1, swap)
    full, mine, away, new = call(
        functools.partial(early_kernel, half),
        "early",
        (b16(rows, wide), b16(rows // 2, wide), b16(rows // 2, wide), f32(2 * kv_heads, group * sub)),
        (pair,),
        idx, meta, query, base, table, f, sf, g1, sg,
        scalars=2,
    )
    there = other_head(away)
    h, full = lax.optimization_barrier((h, full))
    late, late_log = call(
        functools.partial(late_kernel, half),
        "late",
        (b16(sub, wide), f32(kv_heads, group * sub)),
        (),
        idx, meta, query, full, table, new, h,
        scalars=2,
    )
    late_there = other_head(late)
    (log_total,) = call(
        log_kernel, "logs", (f32(kv_heads * group, rows),), (), idx, meta, logs, new, late_log, scalars=2
    )
    chosen = jnp.where(device % 2 == 0, meta[2], meta[0])
    row_sub = head * (QB // 2) + lax.broadcasted_iota(jnp.int32, (rows // 2, 1), 0) // sub
    mine = jnp.where(row_sub == chosen, jnp.concatenate([late] * (QB // 2), axis=0), mine)
    there = jnp.where(row_sub == chosen, jnp.concatenate([late_there] * (QB // 2), axis=0), there)
    attended = jnp.where(
        head == 0,
        jnp.concatenate([mine, there], axis=1),
        jnp.concatenate([there, mine], axis=1),
    )
    return (attended, log_total)


def solution(mesh):
    return jax.shard_map(
        shards,
        mesh=mesh,
        in_specs=(
            P("ctx", "head"),
            P("ctx", "head"),
            P("ctx", "head"),
            P(None, "ctx", "head"),
            P(),
        ),
        out_specs=(P(("ctx", "head"), None), P("head", "ctx")),
        check_vma=False,
    )
```

```python
import functools
import math

import jax
import jax.numpy as jnp
from jax import lax
from jax.experimental import pallas as pl
from jax.experimental.pallas import tpu as pltpu
from jax.sharding import PartitionSpec as P

HD = 128
QB = 4
STEPS = 3
LN2 = math.log(2.0)
FACTOR = 1.0 / (math.sqrt(HD) * LN2)
NEG = -math.inf

SMEM = pl.BlockSpec(memory_space=pltpu.SMEM)
VMEM = pl.BlockSpec(memory_space=pltpu.VMEM)
PARAMS = pltpu.CompilerParams(vmem_limit_bytes=16 * 2**20)
COST = pl.CostEstimate(flops=1000, bytes_accessed=1000, transcendentals=0)


def stacked(q_ref, kv_head, group):
    first = kv_head * group
    return jnp.concatenate([q_ref[:, (first + j) * HD : (first + j + 1) * HD] for j in range(group)], axis=0)


def scores_of(keys, queries):
    return lax.dot_general(keys, queries, (((1,), (1,)), ((), ())), preferred_element_type=jnp.float32)


def mix(left, right):
    return lax.dot_general(left, right, (((0,), (0,)), ((), ())), preferred_element_type=jnp.float32)


def local_kernel(half, entries, idx_ref, plan_ref, q_ref, k_ref, v_ref, held_ref, acc_ref, stat_ref, meta_ref):
    rows = q_ref.shape[0]
    kv_heads = k_ref.shape[1] // HD
    group = q_ref.shape[1] // k_ref.shape[1]
    device = idx_ref[0]
    for t in range(STEPS):
        meta_ref[t] = -1

    def scan(i, carry):
        @pl.when(plan_ref[i, 2] == device)
        def _():
            meta_ref[plan_ref[i, 0]] = plan_ref[i, 3]

        return carry

    lax.fori_loop(0, entries, scan, 0)
    held_bias = jnp.where(device >= half - 2, 0.0, NEG)
    key_pos = lax.broadcasted_iota(jnp.int32, (rows, group * rows), 0)
    row_pos = lax.broadcasted_iota(jnp.int32, (rows, group * rows), 1) % rows
    causal = key_pos <= row_pos
    for g in range(kv_heads):
        cols = slice(g * HD, (g + 1) * HD)
        queries = stacked(q_ref, g, group)
        own = jnp.where(causal, scores_of(k_ref[:, cols], queries), NEG)
        held = scores_of(held_ref[0, :, cols], queries) + held_bias
        top = jnp.maximum(jnp.max(own, axis=0, keepdims=True), jnp.max(held, axis=0, keepdims=True))
        w_own = jnp.exp2((own - top) * FACTOR)
        w_held = jnp.exp2((held - top) * FACTOR)
        stat_ref[g, 0:1, :] = top
        stat_ref[g, 1:2, :] = jnp.sum(w_own, axis=0, keepdims=True) + jnp.sum(w_held, axis=0, keepdims=True)
        acc_ref[g] = mix(v_ref[:, cols], w_own.astype(jnp.bfloat16)) + mix(
            held_ref[1, :, cols], w_held.astype(jnp.bfloat16)
        )


def more(g, q_ref, acc_ref, stat_ref, keys, values, bias):
    group = q_ref.shape[1] // (acc_ref.shape[0] * HD)
    scores = scores_of(keys, stacked(q_ref, g, group)) + bias
    old_top = stat_ref[g, 0:1, :]
    top = jnp.maximum(old_top, jnp.max(scores, axis=0, keepdims=True))
    keep = jnp.exp2((old_top - top) * FACTOR)
    weights = jnp.exp2((scores - top) * FACTOR)
    total = stat_ref[g, 1:2, :] * keep + jnp.sum(weights, axis=0, keepdims=True)
    return top, total, acc_ref[g] * keep + mix(values, weights.astype(jnp.bfloat16))


def two_back_kernel(half, idx_ref, q_ref, acc_ref, stat_ref, n2, out_acc_ref, out_stat_ref):
    bias = jnp.where(idx_ref[0] >= half, 0.0, NEG)
    for g in range(acc_ref.shape[0]):
        cols = slice(g * HD, (g + 1) * HD)
        top, total, mixed = more(g, q_ref, acc_ref, stat_ref, n2[0, :, cols], n2[1, :, cols], bias)
        out_acc_ref[g] = mixed
        out_stat_ref[g, 0:1, :] = top
        out_stat_ref[g, 1:2, :] = total


def near_kernel(half, idx_ref, q_ref, acc_ref, stat_ref, sx, sn2, base_ref, log_ref, sub_ref, kv):
    rows = q_ref.shape[0]
    kv_heads = acc_ref.shape[0]
    group = q_ref.shape[1] // (kv_heads * HD)
    sub = rows // QB
    device = idx_ref[0]
    choose(kv, slice(0, rows), device % 2 == 0, sn2, sx)
    bias = jnp.where(device >= half - 1, 0.0, NEG)
    for g in range(kv_heads):
        cols = slice(g * HD, (g + 1) * HD)
        top, total, mixed = more(g, q_ref, acc_ref, stat_ref, kv[0, :, cols], kv[1, :, cols], bias)
        mixed = mixed * (1.0 / total)
        logs = top * FACTOR + jnp.log2(total)
        for j in range(group):
            lanes = slice(j * rows, (j + 1) * rows)
            at = g * group + j
            base_ref[:, at * HD : (at + 1) * HD] = jnp.transpose(mixed[:, lanes].astype(jnp.bfloat16))
            log_ref[at : at + 1, :] = logs[:, lanes]
        for c in range(QB):
            part = [logs[:, j * rows + c * sub : j * rows + (c + 1) * sub] for j in range(group)]
            sub_ref[c * kv_heads + g : c * kv_heads + g + 1, :] = jnp.concatenate(part, axis=1)


def choose(kv, at, when, one, other):
    @pl.when(when)
    def _():
        kv[:, at, :] = one[...]

    @pl.when(jnp.logical_not(when))
    def _():
        kv[:, at, :] = other[...]


def helped(device, meta_ref):
    even = device % 2 == 0
    return meta_ref[1], jnp.where(even, meta_ref[0], meta_ref[2]), jnp.where(even, meta_ref[2], meta_ref[0])


def update(old_logs, olds, keys, values, queries, bias):
    scores = [scores_of(k, q) * FACTOR for k, q in zip(keys, queries)]
    if bias is not None:
        scores = [s + bias for s in scores]
    tops = [jnp.maximum(o, jnp.max(s, axis=0, keepdims=True)) for o, s in zip(old_logs, scores)]
    weights = [jnp.exp2(s - t) for s, t in zip(scores, tops)]
    keeps = [jnp.exp2(o - t) for o, t in zip(old_logs, tops)]
    totals = [k + jnp.sum(w, axis=0, keepdims=True) for k, w in zip(keeps, weights)]
    inverses = [1.0 / t for t in totals]
    shares = jnp.concatenate([k * i for k, i in zip(keeps, inverses)], axis=0)
    pad = jnp.zeros((8 - shares.shape[0], shares.shape[1]), jnp.float32)
    shares = jnp.transpose(jnp.concatenate([shares, pad], axis=0))
    mixed = [mix((w * i).astype(jnp.bfloat16), v) for w, i, v in zip(weights, inverses, values)]
    outs = [(m + o.astype(jnp.float32) * shares[:, g : g + 1]).astype(jnp.bfloat16) for g, (m, o) in enumerate(zip(mixed, olds))]
    return outs, [t + jnp.log2(n) for t, n in zip(tops, totals)]


def rows_of(ref, starts, names):
    sub = ref.shape[0] // QB
    parts = [ref[pl.ds(pl.multiple_of(c * sub, sub), sub), j * HD : (j + 1) * HD] for c in starts for j in names]
    return jnp.concatenate(parts, axis=0)


def early_kernel(
    half, idx_ref, meta_ref, q_ref, base_ref, sub_ref, f, sf, g1, sg, full_ref, mine_ref, send_ref, new_ref, kv
):
    rows = q_ref.shape[0]
    sub = rows // QB
    kv_heads = f.shape[2] // HD
    group = q_ref.shape[1] // f.shape[2]
    device = idx_ref[0]
    head = idx_ref[1]
    full_ref[...] = base_ref[...]

    @pl.when(device >= half)
    def _():
        choose(kv, slice(0, rows), device == 2 * half - 1, g1, f)
        choose(kv, slice(rows, 2 * rows), device == 2 * half - 2, sg, sf)
        chosen = helped(device, meta_ref)[:2]
        starts = [jnp.maximum(c, 0) for c in chosen]
        lanes = group * sub
        first_key = lax.broadcasted_iota(jnp.int32, (2 * rows, 2 * lanes), 0) < rows
        first_row = lax.broadcasted_iota(jnp.int32, (2 * rows, 2 * lanes), 1) < lanes
        bias = jnp.where(first_key == first_row, 0.0, jnp.where(chosen[0] == chosen[1], 0.0, NEG))
        names = [range(g * group, (g + 1) * group) for g in range(kv_heads)]
        cols = [slice(g * HD, (g + 1) * HD) for g in range(kv_heads)]
        finals, logs = update(
            [
                jnp.concatenate([sub_ref[pl.ds(c * kv_heads + g, 1), :] for c in starts], axis=1)
                for g in range(kv_heads)
            ],
            [rows_of(base_ref, starts, n) for n in names],
            [kv[0, :, c] for c in cols],
            [kv[1, :, c] for c in cols],
            [rows_of(q_ref, starts, n) for n in names],
            bias,
        )
        for slot in range(2):
            at_rows = pl.ds(pl.multiple_of(starts[slot] * sub, sub), sub)
            for g in range(kv_heads):
                new_ref[slot * kv_heads + g : slot * kv_heads + g + 1, :] = logs[g][:, slot * lanes : (slot + 1) * lanes]

            @pl.when(chosen[slot] >= 0)
            def _():
                for g in range(kv_heads):
                    for i, j in enumerate(names[g]):
                        at = slot * lanes + i * sub
                        full_ref[at_rows, j * HD : (j + 1) * HD] = finals[g][at : at + sub]

    half_rows = rows // 2
    mine_ref[...] = full_ref[pl.ds(pl.multiple_of(head * half_rows, half_rows), half_rows), :]
    send_ref[...] = full_ref[pl.ds(pl.multiple_of((1 - head) * half_rows, half_rows), half_rows), :]


def late_kernel(half, idx_ref, meta_ref, q_ref, full_ref, table_ref, new_ref, h, late_ref, log_ref):
    rows = q_ref.shape[0]
    sub = rows // QB
    kv_heads = h.shape[2] // HD
    group = q_ref.shape[1] // h.shape[2]
    first, second, chosen = helped(idx_ref[0], meta_ref)

    @pl.when(chosen >= 0)
    def _():
        names = [range(g * group, (g + 1) * group) for g in range(kv_heads)]
        cols = [slice(g * HD, (g + 1) * HD) for g in range(kv_heads)]
        old_logs = []
        for g in range(kv_heads):
            old_log = table_ref[pl.ds(chosen * kv_heads + g, 1), :]
            old_log = jnp.where(first == chosen, new_ref[g : g + 1, :], old_log)
            old_logs.append(jnp.where(second == chosen, new_ref[kv_heads + g : kv_heads + g + 1, :], old_log))
        finals, logs = update(
            old_logs,
            [rows_of(full_ref, [chosen], n) for n in names],
            [h[0, :, c] for c in cols],
            [h[1, :, c] for c in cols],
            [rows_of(q_ref, [chosen], n) for n in names],
            None,
        )
        for g in range(kv_heads):
            log_ref[g : g + 1, :] = logs[g]
            for i, j in enumerate(names[g]):
                late_ref[:, j * HD : (j + 1) * HD] = finals[g][i * sub : (i + 1) * sub]


def log_kernel(slots, scale, idx_ref, meta_ref, old_ref, new_ref, log_ref):
    heads, rows = log_ref.shape
    kv_heads = new_ref.shape[0] // len(slots)
    group = heads // kv_heads
    sub = rows // QB
    row_sub = lax.broadcasted_iota(jnp.int32, (1, rows), 1) // sub
    results = [old_ref[j : j + 1, :] for j in range(heads)]
    for at, slot in enumerate(slots):
        chosen = helped(idx_ref[0], meta_ref)[slot]
        source = new_ref[at * kv_heads : (at + 1) * kv_heads, :]
        for i in range(group):
            moved = pltpu.roll(source, (chosen + QB - i) % QB * sub, 1)
            for g in range(kv_heads):
                j = g * group + i
                results[j] = jnp.where(row_sub == chosen, moved[g : g + 1, :], results[j])
    for j in range(heads):
        log_ref[j : j + 1, :] = results[j] * scale


def call(kernel, name, outs, scratch, *args, scalars):
    return pl.pallas_call(
        kernel,
        out_shape=outs,
        in_specs=[SMEM] * scalars + [VMEM] * (len(args) - scalars),
        out_specs=[SMEM if out.shape == (STEPS,) else VMEM for out in outs],
        scratch_shapes=scratch,
        compiler_params=PARAMS,
        cost_estimate=COST,
        name=name,
    )(*args)


def shards(query, key, value, held_kv, plan):
    rows = query.shape[0]
    sub = rows // QB
    wide = query.shape[1]
    kv_heads = key.shape[1] // HD
    group = wide // key.shape[1]
    size = lax.axis_size("ctx")
    half = size // 2
    device = lax.axis_index("ctx")
    head = lax.axis_index("head")
    idx = jnp.stack([device, head]).astype(jnp.int32)

    def send(x, route):
        return lax.ppermute(x, "ctx", route)

    def other_head(x):
        return lax.ppermute(x, "head", [(0, 1), (1, 0)])

    def f32(*shape):
        return jax.ShapeDtypeStruct(shape, jnp.float32)

    def b16(*shape):
        return jax.ShapeDtypeStruct(shape, jnp.bfloat16)

    swap = [(i, i ^ 1) for i in range(size)]
    two_on = swap[: half - 2] + [(i, i + 2) for i in range(half - 2, size - 2)]
    two_on += [(i, i - half) for i in range(size - 2, size)]
    across = [(i, i + half + 1) for i in range(half - 2)] + swap[half - 2 : half]
    across += [(i, i - half) for i in range(half, size - 2)] + [(size - 2, size - 1), (size - 1, half)]
    extra = [(half - 2, size - 1), (size - 1, size - 2), (size - 2, half - 1), (half - 1, half - 2)]
    moved = {i for i, _ in extra}
    extra += [(i, j) for i, j in swap if i not in moved]
    beside = swap[:half] + [(i, half + (i - half + (1 if i % 2 else -1)) % half) for i in range(half, size)]

    n2 = send(held_kv, two_on)
    sx = send(held_kv, swap)
    f = send(held_kv, across)
    acc, stat, meta = call(
        functools.partial(local_kernel, half, plan.shape[0]),
        "local",
        (f32(kv_heads, HD, group * rows), f32(kv_heads, 2, group * rows), jax.ShapeDtypeStruct((STEPS,), jnp.int32)),
        (),
        idx, plan, query, key, value, held_kv,
        scalars=2,
    )
    held_late, acc = lax.optimization_barrier((held_kv, acc))
    g1 = send(held_late, extra)
    pair = pltpu.VMEM((2, 2 * rows, key.shape[1]), jnp.bfloat16)
    outs = (b16(rows, wide), f32(kv_heads * group, rows), f32(QB * kv_heads, group * sub))
    state = (f32(kv_heads, HD, group * rows), f32(kv_heads, 2, group * rows))
    held_late, acc = lax.optimization_barrier((held_kv, acc))
    g1 = send(held_late, extra)
    chosen = jnp.where(device % 2 == 0, meta[2], meta[0]) - head * (QB // 2)
    row_sub = lax.broadcasted_iota(jnp.int32, (rows // 2, 1), 0) // sub
    n2, acc, chosen = lax.optimization_barrier((n2, acc, chosen))

    def near(n2, sx, acc, stat):
        sn2 = send(n2, swap)
        acc, stat = call(
            functools.partial(two_back_kernel, half), "two_back", state, (), idx, query, acc, stat, n2, scalars=1
        )
        one = pltpu.VMEM(held_kv.shape, jnp.bfloat16)
        return list(
            call(functools.partial(near_kernel, half), "near", outs, (one,), idx, query, acc, stat, sx, sn2, scalars=1)
        )

    def none(n2, sx, acc, stat):
        return [jnp.zeros(out.shape, out.dtype) for out in outs]

    base, logs, table = lax.cond(plan[0, 0] >= 0, near, none, n2, sx, acc, stat)
    f, base = lax.optimization_barrier((f, base))
    h = send(f, beside)
    sf = send(f, swap)
    sg = send(g1, swap)
    full, mine, away, new = call(
        functools.partial(early_kernel, half),
        "early",
        (b16(rows, wide), b16(rows // 2, wide), b16(rows // 2, wide), f32(2 * kv_heads, group * sub)),
        (pair,),
        idx, meta, query, base, table, f, sf, g1, sg,
        scalars=2,
    )
    there = other_head(away)
    log_out = f32(kv_heads * group, rows)
    (logs,) = call(functools.partial(log_kernel, (0, 1), 1.0), "logs", (log_out,), (), idx, meta, logs, new, scalars=2)
    h, full, logs = lax.optimization_barrier((h, full, logs))
    late, late_log = call(
        functools.partial(late_kernel, half),
        "late",
        (b16(sub, wide), f32(kv_heads, group * sub)),
        (),
        idx, meta, query, full, table, new, h,
        scalars=2,
    )
    late_there = other_head(late)
    (log_total,) = call(
        functools.partial(log_kernel, (2,), LN2), "last_logs", (log_out,), (), idx, meta, logs, late_log, scalars=2
    )
    in_late = row_sub == chosen
    mine = jnp.where(in_late, jnp.concatenate([late] * (QB // 2), axis=0), mine)
    there = jnp.where(in_late, jnp.concatenate([late_there] * (QB // 2), axis=0), there)
    attended = jnp.where(
        head == 0,
        jnp.concatenate([mine, there], axis=1),
        jnp.concatenate([there, mine], axis=1),
    )
    return (attended, log_total)


def solution(mesh):
    return jax.shard_map(
        shards,
        mesh=mesh,
        in_specs=(
            P("ctx", "head"),
            P("ctx", "head"),
            P("ctx", "head"),
            P(None, "ctx", "head"),
            P(),
        ),
        out_specs=(P(("ctx", "head"), None), P("head", "ctx")),
        check_vma=False,
    )
```

```python
import functools
import math

import jax
import jax.numpy as jnp
from jax import lax
from jax.experimental import pallas as pl
from jax.experimental.pallas import tpu as pltpu
from jax.sharding import PartitionSpec as P

HD = 128
QB = 4
STEPS = 3
LN2 = math.log(2.0)
FACTOR = 1.0 / (math.sqrt(HD) * LN2)
NEG = -math.inf

SMEM = pl.BlockSpec(memory_space=pltpu.SMEM)
VMEM = pl.BlockSpec(memory_space=pltpu.VMEM)
PARAMS = pltpu.CompilerParams(vmem_limit_bytes=16 * 2**20)
COST = pl.CostEstimate(flops=1000, bytes_accessed=1000, transcendentals=0)


def stacked(q_ref, kv_head, group):
    first = kv_head * group
    return jnp.concatenate([q_ref[:, (first + j) * HD : (first + j + 1) * HD] for j in range(group)], axis=0)


def scores_of(keys, queries):
    return lax.dot_general(keys, queries, (((1,), (1,)), ((), ())), preferred_element_type=jnp.float32)


def mix(left, right):
    return lax.dot_general(left, right, (((0,), (0,)), ((), ())), preferred_element_type=jnp.float32)


def local_kernel(half, entries, idx_ref, plan_ref, q_ref, k_ref, v_ref, held_ref, acc_ref, stat_ref, meta_ref):
    rows = q_ref.shape[0]
    kv_heads = k_ref.shape[1] // HD
    group = q_ref.shape[1] // k_ref.shape[1]
    device = idx_ref[0]
    for t in range(STEPS):
        meta_ref[t] = -1

    def scan(i, carry):
        @pl.when(plan_ref[i, 2] == device)
        def _():
            meta_ref[plan_ref[i, 0]] = plan_ref[i, 3]

        return carry

    lax.fori_loop(0, entries, scan, 0)
    held_bias = jnp.where(device >= half - 2, 0.0, NEG)
    key_pos = lax.broadcasted_iota(jnp.int32, (rows, group * rows), 0)
    row_pos = lax.broadcasted_iota(jnp.int32, (rows, group * rows), 1) % rows
    causal = key_pos <= row_pos
    for g in range(kv_heads):
        cols = slice(g * HD, (g + 1) * HD)
        queries = stacked(q_ref, g, group)
        own = jnp.where(causal, scores_of(k_ref[:, cols], queries), NEG)
        held = scores_of(held_ref[0, :, cols], queries) + held_bias
        top = jnp.maximum(jnp.max(own, axis=0, keepdims=True), jnp.max(held, axis=0, keepdims=True))
        w_own = jnp.exp2((own - top) * FACTOR)
        w_held = jnp.exp2((held - top) * FACTOR)
        stat_ref[g, 0:1, :] = top
        stat_ref[g, 1:2, :] = jnp.sum(w_own, axis=0, keepdims=True) + jnp.sum(w_held, axis=0, keepdims=True)
        acc_ref[g] = mix(v_ref[:, cols], w_own.astype(jnp.bfloat16)) + mix(
            held_ref[1, :, cols], w_held.astype(jnp.bfloat16)
        )


def last_sent(device, head, meta_ref):
    chosen = helped(device, meta_ref)[2] - (1 - head) * (QB // 2)
    return jnp.where((chosen >= 0) & (chosen < QB // 2), chosen, 1)


def more(g, q_ref, acc_ref, stat_ref, keys, values, bias):
    group = q_ref.shape[1] // (acc_ref.shape[0] * HD)
    scores = scores_of(keys, stacked(q_ref, g, group)) + bias
    old_top = stat_ref[g, 0:1, :]
    top = jnp.maximum(old_top, jnp.max(scores, axis=0, keepdims=True))
    keep = jnp.exp2((old_top - top) * FACTOR)
    weights = jnp.exp2((scores - top) * FACTOR)
    total = stat_ref[g, 1:2, :] * keep + jnp.sum(weights, axis=0, keepdims=True)
    return top, total, acc_ref[g] * keep + mix(values, weights.astype(jnp.bfloat16))


def two_back_kernel(half, idx_ref, q_ref, acc_ref, stat_ref, n2, out_acc_ref, out_stat_ref):
    bias = jnp.where(idx_ref[0] >= half, 0.0, NEG)
    for g in range(acc_ref.shape[0]):
        cols = slice(g * HD, (g + 1) * HD)
        top, total, mixed = more(g, q_ref, acc_ref, stat_ref, n2[0, :, cols], n2[1, :, cols], bias)
        out_acc_ref[g] = mixed
        out_stat_ref[g, 0:1, :] = top
        out_stat_ref[g, 1:2, :] = total


def near_kernel(half, idx_ref, q_ref, acc_ref, stat_ref, sx, sn2, base_ref, log_ref, sub_ref, kv):
    rows = q_ref.shape[0]
    kv_heads = acc_ref.shape[0]
    group = q_ref.shape[1] // (kv_heads * HD)
    sub = rows // QB
    device = idx_ref[0]
    choose(kv, slice(0, rows), device % 2 == 0, sn2, sx)
    bias = jnp.where(device >= half - 1, 0.0, NEG)
    for g in range(kv_heads):
        cols = slice(g * HD, (g + 1) * HD)
        top, total, mixed = more(g, q_ref, acc_ref, stat_ref, kv[0, :, cols], kv[1, :, cols], bias)
        mixed = mixed * (1.0 / total)
        logs = top * FACTOR + jnp.log2(total)
        for j in range(group):
            lanes = slice(j * rows, (j + 1) * rows)
            at = g * group + j
            base_ref[:, at * HD : (at + 1) * HD] = jnp.transpose(mixed[:, lanes].astype(jnp.bfloat16))
            log_ref[at : at + 1, :] = logs[:, lanes]
        for c in range(QB):
            part = [logs[:, j * rows + c * sub : j * rows + (c + 1) * sub] for j in range(group)]
            sub_ref[c * kv_heads + g : c * kv_heads + g + 1, :] = jnp.concatenate(part, axis=1)


def choose(kv, at, when, one, other):
    @pl.when(when)
    def _():
        kv[:, at, :] = one[...]

    @pl.when(jnp.logical_not(when))
    def _():
        kv[:, at, :] = other[...]


def helped(device, meta_ref):
    even = device % 2 == 0
    return meta_ref[1], jnp.where(even, meta_ref[0], meta_ref[2]), jnp.where(even, meta_ref[2], meta_ref[0])


def update(old_logs, olds, keys, values, queries, bias):
    scores = [scores_of(k, q) * FACTOR for k, q in zip(keys, queries)]
    if bias is not None:
        scores = [s + bias for s in scores]
    tops = [jnp.maximum(o, jnp.max(s, axis=0, keepdims=True)) for o, s in zip(old_logs, scores)]
    weights = [jnp.exp2(s - t) for s, t in zip(scores, tops)]
    keeps = [jnp.exp2(o - t) for o, t in zip(old_logs, tops)]
    totals = [k + jnp.sum(w, axis=0, keepdims=True) for k, w in zip(keeps, weights)]
    inverses = [1.0 / t for t in totals]
    shares = jnp.concatenate([k * i for k, i in zip(keeps, inverses)], axis=0)
    pad = jnp.zeros((8 - shares.shape[0], shares.shape[1]), jnp.float32)
    shares = jnp.transpose(jnp.concatenate([shares, pad], axis=0))
    mixed = [mix((w * i).astype(jnp.bfloat16), v) for w, i, v in zip(weights, inverses, values)]
    outs = [(m + o.astype(jnp.float32) * shares[:, g : g + 1]).astype(jnp.bfloat16) for g, (m, o) in enumerate(zip(mixed, olds))]
    return outs, [t + jnp.log2(n) for t, n in zip(tops, totals)]


def rows_of(ref, starts, names):
    sub = ref.shape[0] // QB
    parts = [ref[pl.ds(pl.multiple_of(c * sub, sub), sub), j * HD : (j + 1) * HD] for c in starts for j in names]
    return jnp.concatenate(parts, axis=0)


def early_kernel(
    half, idx_ref, meta_ref, q_ref, base_ref, sub_ref, f, sf, g1, sg, full_ref, mine_ref, send_ref, new_ref, kv
):
    rows = q_ref.shape[0]
    sub = rows // QB
    kv_heads = f.shape[2] // HD
    group = q_ref.shape[1] // f.shape[2]
    device = idx_ref[0]
    head = idx_ref[1]
    full_ref[...] = base_ref[...]

    @pl.when(device >= half)
    def _():
        choose(kv, slice(0, rows), device == 2 * half - 1, g1, f)
        choose(kv, slice(rows, 2 * rows), device == 2 * half - 2, sg, sf)
        chosen = helped(device, meta_ref)[:2]
        starts = [jnp.maximum(c, 0) for c in chosen]
        lanes = group * sub
        first_key = lax.broadcasted_iota(jnp.int32, (2 * rows, 2 * lanes), 0) < rows
        first_row = lax.broadcasted_iota(jnp.int32, (2 * rows, 2 * lanes), 1) < lanes
        bias = jnp.where(first_key == first_row, 0.0, jnp.where(chosen[0] == chosen[1], 0.0, NEG))
        names = [range(g * group, (g + 1) * group) for g in range(kv_heads)]
        cols = [slice(g * HD, (g + 1) * HD) for g in range(kv_heads)]
        finals, logs = update(
            [
                jnp.concatenate([sub_ref[pl.ds(c * kv_heads + g, 1), :] for c in starts], axis=1)
                for g in range(kv_heads)
            ],
            [rows_of(base_ref, starts, n) for n in names],
            [kv[0, :, c] for c in cols],
            [kv[1, :, c] for c in cols],
            [rows_of(q_ref, starts, n) for n in names],
            bias,
        )
        for slot in range(2):
            at_rows = pl.ds(pl.multiple_of(starts[slot] * sub, sub), sub)
            for g in range(kv_heads):
                new_ref[slot * kv_heads + g : slot * kv_heads + g + 1, :] = logs[g][:, slot * lanes : (slot + 1) * lanes]

            @pl.when(chosen[slot] >= 0)
            def _():
                for g in range(kv_heads):
                    for i, j in enumerate(names[g]):
                        at = slot * lanes + i * sub
                        full_ref[at_rows, j * HD : (j + 1) * HD] = finals[g][at : at + sub]

    half_rows = rows // 2
    mine_ref[...] = full_ref[pl.ds(pl.multiple_of(head * half_rows, half_rows), half_rows), :]
    first = (1 - last_sent(device, head, meta_ref)) * sub + (1 - head) * half_rows
    send_ref[...] = full_ref[pl.ds(pl.multiple_of(first, sub), sub), :]


def late_kernel(half, idx_ref, meta_ref, q_ref, full_ref, table_ref, new_ref, h, late_ref, send_ref, log_ref):
    rows = q_ref.shape[0]
    sub = rows // QB
    kv_heads = h.shape[2] // HD
    group = q_ref.shape[1] // h.shape[2]
    device = idx_ref[0]
    head = idx_ref[1]
    first, second, chosen = helped(device, meta_ref)
    at_send = last_sent(device, head, meta_ref) * sub + (1 - head) * (rows // 2)
    send_ref[...] = full_ref[pl.ds(pl.multiple_of(at_send, sub), sub), :]

    @pl.when(chosen >= 0)
    def _():
        names = [range(g * group, (g + 1) * group) for g in range(kv_heads)]
        cols = [slice(g * HD, (g + 1) * HD) for g in range(kv_heads)]
        old_logs = []
        for g in range(kv_heads):
            old_log = table_ref[pl.ds(chosen * kv_heads + g, 1), :]
            old_log = jnp.where(first == chosen, new_ref[g : g + 1, :], old_log)
            old_logs.append(jnp.where(second == chosen, new_ref[kv_heads + g : kv_heads + g + 1, :], old_log))
        finals, logs = update(
            old_logs,
            [rows_of(full_ref, [chosen], n) for n in names],
            [h[0, :, c] for c in cols],
            [h[1, :, c] for c in cols],
            [rows_of(q_ref, [chosen], n) for n in names],
            None,
        )
        for g in range(kv_heads):
            log_ref[g : g + 1, :] = logs[g]
        here = chosen // (QB // 2) == head

        @pl.when(here)
        def _():
            for g in range(kv_heads):
                for i, j in enumerate(names[g]):
                    late_ref[:, j * HD : (j + 1) * HD] = finals[g][i * sub : (i + 1) * sub]

        @pl.when(jnp.logical_not(here))
        def _():
            for g in range(kv_heads):
                for i, j in enumerate(names[g]):
                    send_ref[:, j * HD : (j + 1) * HD] = finals[g][i * sub : (i + 1) * sub]


def log_kernel(slots, scale, idx_ref, meta_ref, old_ref, new_ref, log_ref):
    heads, rows = log_ref.shape
    kv_heads = new_ref.shape[0] // len(slots)
    group = heads // kv_heads
    sub = rows // QB
    row_sub = lax.broadcasted_iota(jnp.int32, (1, rows), 1) // sub
    results = [old_ref[j : j + 1, :] for j in range(heads)]
    for at, slot in enumerate(slots):
        chosen = helped(idx_ref[0], meta_ref)[slot]
        source = new_ref[at * kv_heads : (at + 1) * kv_heads, :]
        for i in range(group):
            moved = pltpu.roll(source, (chosen + QB - i) % QB * sub, 1)
            for g in range(kv_heads):
                j = g * group + i
                results[j] = jnp.where(row_sub == chosen, moved[g : g + 1, :], results[j])
    for j in range(heads):
        log_ref[j : j + 1, :] = results[j] * scale


def call(kernel, name, outs, scratch, *args, scalars):
    return pl.pallas_call(
        kernel,
        out_shape=outs,
        in_specs=[SMEM] * scalars + [VMEM] * (len(args) - scalars),
        out_specs=[SMEM if out.shape == (STEPS,) else VMEM for out in outs],
        scratch_shapes=scratch,
        compiler_params=PARAMS,
        cost_estimate=COST,
        name=name,
    )(*args)


def shards(query, key, value, held_kv, plan):
    rows = query.shape[0]
    sub = rows // QB
    wide = query.shape[1]
    kv_heads = key.shape[1] // HD
    group = wide // key.shape[1]
    size = lax.axis_size("ctx")
    half = size // 2
    device = lax.axis_index("ctx")
    head = lax.axis_index("head")
    idx = jnp.stack([device, head]).astype(jnp.int32)

    def send(x, route):
        return lax.ppermute(x, "ctx", route)

    def other_head(x):
        return lax.ppermute(x, "head", [(0, 1), (1, 0)])

    def f32(*shape):
        return jax.ShapeDtypeStruct(shape, jnp.float32)

    def b16(*shape):
        return jax.ShapeDtypeStruct(shape, jnp.bfloat16)

    swap = [(i, i ^ 1) for i in range(size)]
    two_on = swap[: half - 2] + [(i, i + 2) for i in range(half - 2, size - 2)]
    two_on += [(i, i - half) for i in range(size - 2, size)]
    across = [(i, i + half + 1) for i in range(half - 2)] + swap[half - 2 : half]
    across += [(i, i - half) for i in range(half, size - 2)] + [(size - 2, size - 1), (size - 1, half)]
    extra = [(half - 2, size - 1), (size - 1, size - 2), (size - 2, half - 1), (half - 1, half - 2)]
    moved = {i for i, _ in extra}
    extra += [(i, j) for i, j in swap if i not in moved]
    beside = swap[:half] + [(i, half + (i - half + (1 if i % 2 else -1)) % half) for i in range(half, size)]

    n2 = send(held_kv, two_on)
    sx = send(held_kv, swap)
    f = send(held_kv, across)
    acc, stat, meta = call(
        functools.partial(local_kernel, half, plan.shape[0]),
        "local",
        (f32(kv_heads, HD, group * rows), f32(kv_heads, 2, group * rows), jax.ShapeDtypeStruct((STEPS,), jnp.int32)),
        (),
        idx, plan, query, key, value, held_kv,
        scalars=2,
    )
    held_late, acc = lax.optimization_barrier((held_kv, acc))
    g1 = send(held_late, extra)
    pair = pltpu.VMEM((2, 2 * rows, key.shape[1]), jnp.bfloat16)
    outs = (b16(rows, wide), f32(kv_heads * group, rows), f32(QB * kv_heads, group * sub))
    state = (f32(kv_heads, HD, group * rows), f32(kv_heads, 2, group * rows))
    held_late, acc = lax.optimization_barrier((held_kv, acc))
    g1 = send(held_late, extra)
    chosen = jnp.where(device % 2 == 0, meta[2], meta[0]) - head * (QB // 2)
    row_sub = lax.broadcasted_iota(jnp.int32, (rows // 2, 1), 0) // sub
    last = jnp.where((chosen >= 0) & (chosen < QB // 2), chosen, 1)
    n2, acc, chosen, last = lax.optimization_barrier((n2, acc, chosen, last))

    def two_back(n2, acc, stat):
        sn2 = send(n2, swap)
        args = (idx, query, acc, stat, n2)
        return [sn2, *call(functools.partial(two_back_kernel, half), "two_back", state, (), *args, scalars=1)]

    def none(n2, acc, stat):
        return [n2, acc, stat]

    sn2, acc, stat = lax.cond(plan[0, 0] >= 0, two_back, none, n2, acc, stat)
    f, acc = lax.optimization_barrier((f, acc))
    h = send(f, beside)
    sf = send(f, swap)
    sg = send(g1, swap)
    one = pltpu.VMEM(held_kv.shape, jnp.bfloat16)
    base, logs, table = call(
        functools.partial(near_kernel, half), "near", outs, (one,), idx, query, acc, stat, sx, sn2, scalars=1
    )
    full, mine, away, new = call(
        functools.partial(early_kernel, half),
        "early",
        (b16(rows, wide), b16(rows // 2, wide), b16(sub, wide), f32(2 * kv_heads, group * sub)),
        (pair,),
        idx, meta, query, base, table, f, sf, g1, sg,
        scalars=2,
    )
    there = other_head(away)
    log_out = f32(kv_heads * group, rows)
    (logs,) = call(functools.partial(log_kernel, (0, 1), 1.0), "logs", (log_out,), (), idx, meta, logs, new, scalars=2)
    h, full, logs = lax.optimization_barrier((h, full, logs))
    late, late_away, late_log = call(
        functools.partial(late_kernel, half),
        "late",
        (b16(sub, wide), b16(sub, wide), f32(kv_heads, group * sub)),
        (),
        idx, meta, query, full, table, new, h,
        scalars=2,
    )
    late_away, there = lax.optimization_barrier((late_away, there))
    late_there = other_head(late_away)
    (log_total,) = call(
        functools.partial(log_kernel, (2,), LN2), "last_logs", (log_out,), (), idx, meta, logs, late_log, scalars=2
    )
    mine = jnp.where(row_sub == chosen, jnp.concatenate([late] * (QB // 2), axis=0), mine)
    there = jnp.where(
        row_sub == last,
        jnp.concatenate([late_there] * (QB // 2), axis=0),
        jnp.concatenate([there] * (QB // 2), axis=0),
    )
    attended = jnp.where(
        head == 0,
        jnp.concatenate([mine, there], axis=1),
        jnp.concatenate([there, mine], axis=1),
    )
    return (attended, log_total)


def solution(mesh):
    return jax.shard_map(
        shards,
        mesh=mesh,
        in_specs=(
            P("ctx", "head"),
            P("ctx", "head"),
            P("ctx", "head"),
            P(None, "ctx", "head"),
            P(),
        ),
        out_specs=(P(("ctx", "head"), None), P("head", "ctx")),
        check_vma=False,
    )
```

```python
import functools
import math

import jax
import jax.numpy as jnp
from jax import lax
from jax.experimental import pallas as pl
from jax.experimental.pallas import tpu as pltpu
from jax.sharding import PartitionSpec as P

HD = 128
QB = 4
STEPS = 3
LN2 = math.log(2.0)
FACTOR = 1.0 / (math.sqrt(HD) * LN2)
NEG = -math.inf

SMEM = pl.BlockSpec(memory_space=pltpu.SMEM)
VMEM = pl.BlockSpec(memory_space=pltpu.VMEM)
PARAMS = pltpu.CompilerParams(vmem_limit_bytes=16 * 2**20)
COST = pl.CostEstimate(flops=1000, bytes_accessed=1000, transcendentals=0)


def stacked(q_ref, kv_head, group):
    first = kv_head * group
    return jnp.concatenate([q_ref[:, (first + j) * HD : (first + j + 1) * HD] for j in range(group)], axis=0)


def scores_of(keys, queries):
    return lax.dot_general(keys, queries, (((1,), (1,)), ((), ())), preferred_element_type=jnp.float32)


def mix(left, right):
    return lax.dot_general(left, right, (((0,), (0,)), ((), ())), preferred_element_type=jnp.float32)


def local_kernel(half, entries, idx_ref, plan_ref, q_ref, k_ref, v_ref, held_ref, acc_ref, stat_ref, meta_ref):
    rows = q_ref.shape[0]
    kv_heads = k_ref.shape[1] // HD
    group = q_ref.shape[1] // k_ref.shape[1]
    device = idx_ref[0]
    for t in range(STEPS):
        meta_ref[t] = -1

    def scan(i, carry):
        @pl.when(plan_ref[i, 2] == device)
        def _():
            meta_ref[plan_ref[i, 0]] = plan_ref[i, 3]

        return carry

    lax.fori_loop(0, entries, scan, 0)
    held_bias = jnp.where(device >= half - 2, 0.0, NEG)
    key_pos = lax.broadcasted_iota(jnp.int32, (rows, group * rows), 0)
    row_pos = lax.broadcasted_iota(jnp.int32, (rows, group * rows), 1) % rows
    causal = key_pos <= row_pos
    for g in range(kv_heads):
        cols = slice(g * HD, (g + 1) * HD)
        queries = stacked(q_ref, g, group)
        own = jnp.where(causal, scores_of(k_ref[:, cols], queries), NEG)
        held = scores_of(held_ref[0, :, cols], queries) + held_bias
        top = jnp.maximum(jnp.max(own, axis=0, keepdims=True), jnp.max(held, axis=0, keepdims=True))
        w_own = jnp.exp2((own - top) * FACTOR)
        w_held = jnp.exp2((held - top) * FACTOR)
        stat_ref[g, 0:1, :] = top
        stat_ref[g, 1:2, :] = jnp.sum(w_own, axis=0, keepdims=True) + jnp.sum(w_held, axis=0, keepdims=True)
        acc_ref[g] = mix(v_ref[:, cols], w_own.astype(jnp.bfloat16)) + mix(
            held_ref[1, :, cols], w_held.astype(jnp.bfloat16)
        )


def last_sent(device, head, meta_ref):
    chosen = helped(device, meta_ref)[2] - (1 - head) * (QB // 2)
    return jnp.where((chosen >= 0) & (chosen < QB // 2), chosen, 1)


def more(g, q_ref, acc_ref, stat_ref, keys, values, bias):
    group = q_ref.shape[1] // (acc_ref.shape[0] * HD)
    scores = scores_of(keys, stacked(q_ref, g, group)) + bias
    old_top = stat_ref[g, 0:1, :]
    top = jnp.maximum(old_top, jnp.max(scores, axis=0, keepdims=True))
    keep = jnp.exp2((old_top - top) * FACTOR)
    weights = jnp.exp2((scores - top) * FACTOR)
    total = stat_ref[g, 1:2, :] * keep + jnp.sum(weights, axis=0, keepdims=True)
    return top, total, acc_ref[g] * keep + mix(values, weights.astype(jnp.bfloat16))


def two_back_kernel(half, idx_ref, q_ref, acc_ref, stat_ref, n2, out_acc_ref, out_stat_ref):
    bias = jnp.where(idx_ref[0] >= half, 0.0, NEG)
    for g in range(acc_ref.shape[0]):
        cols = slice(g * HD, (g + 1) * HD)
        top, total, mixed = more(g, q_ref, acc_ref, stat_ref, n2[0, :, cols], n2[1, :, cols], bias)
        out_acc_ref[g] = mixed
        out_stat_ref[g, 0:1, :] = top
        out_stat_ref[g, 1:2, :] = total


def near_kernel(half, idx_ref, q_ref, acc_ref, stat_ref, sx, sn2, base_ref, log_ref, sub_ref, kv):
    rows = q_ref.shape[0]
    kv_heads = acc_ref.shape[0]
    group = q_ref.shape[1] // (kv_heads * HD)
    sub = rows // QB
    device = idx_ref[0]
    choose(kv, slice(0, rows), device % 2 == 0, sn2, sx)
    bias = jnp.where(device >= half - 1, 0.0, NEG)
    for g in range(kv_heads):
        cols = slice(g * HD, (g + 1) * HD)
        top, total, mixed = more(g, q_ref, acc_ref, stat_ref, kv[0, :, cols], kv[1, :, cols], bias)
        mixed = mixed * (1.0 / total)
        logs = top * FACTOR + jnp.log2(total)
        for j in range(group):
            lanes = slice(j * rows, (j + 1) * rows)
            at = g * group + j
            base_ref[:, at * HD : (at + 1) * HD] = jnp.transpose(mixed[:, lanes].astype(jnp.bfloat16))
            log_ref[at : at + 1, :] = logs[:, lanes]
        for c in range(QB):
            part = [logs[:, j * rows + c * sub : j * rows + (c + 1) * sub] for j in range(group)]
            sub_ref[c * kv_heads + g : c * kv_heads + g + 1, :] = jnp.concatenate(part, axis=1)


def choose(kv, at, when, one, other):
    @pl.when(when)
    def _():
        kv[:, at, :] = one[...]

    @pl.when(jnp.logical_not(when))
    def _():
        kv[:, at, :] = other[...]


def helped(device, meta_ref):
    even = device % 2 == 0
    return meta_ref[1], jnp.where(even, meta_ref[0], meta_ref[2]), jnp.where(even, meta_ref[2], meta_ref[0])


def update(old_logs, olds, keys, values, queries, bias):
    scores = [scores_of(k, q) * FACTOR for k, q in zip(keys, queries)]
    if bias is not None:
        scores = [s + bias for s in scores]
    tops = [jnp.maximum(o, jnp.max(s, axis=0, keepdims=True)) for o, s in zip(old_logs, scores)]
    weights = [jnp.exp2(s - t) for s, t in zip(scores, tops)]
    keeps = [jnp.exp2(o - t) for o, t in zip(old_logs, tops)]
    totals = [k + jnp.sum(w, axis=0, keepdims=True) for k, w in zip(keeps, weights)]
    inverses = [1.0 / t for t in totals]
    shares = jnp.concatenate([k * i for k, i in zip(keeps, inverses)], axis=0)
    pad = jnp.zeros((8 - shares.shape[0], shares.shape[1]), jnp.float32)
    shares = jnp.transpose(jnp.concatenate([shares, pad], axis=0))
    mixed = [mix((w * i).astype(jnp.bfloat16), v) for w, i, v in zip(weights, inverses, values)]
    outs = [(m + o.astype(jnp.float32) * shares[:, g : g + 1]).astype(jnp.bfloat16) for g, (m, o) in enumerate(zip(mixed, olds))]
    return outs, [t + jnp.log2(n) for t, n in zip(tops, totals)]


def rows_of(ref, starts, names):
    sub = ref.shape[0] // QB
    parts = [ref[pl.ds(pl.multiple_of(c * sub, sub), sub), j * HD : (j + 1) * HD] for c in starts for j in names]
    return jnp.concatenate(parts, axis=0)


def early_kernel(
    half, idx_ref, meta_ref, q_ref, base_ref, sub_ref, f, sf, g1, sg, full_ref, mine_ref, send_ref, new_ref, kv
):
    rows = q_ref.shape[0]
    sub = rows // QB
    kv_heads = f.shape[2] // HD
    group = q_ref.shape[1] // f.shape[2]
    device = idx_ref[0]
    head = idx_ref[1]
    full_ref[...] = base_ref[...]

    @pl.when(device >= half)
    def _():
        choose(kv, slice(0, rows), device == 2 * half - 1, g1, f)
        choose(kv, slice(rows, 2 * rows), device == 2 * half - 2, sg, sf)
        chosen = helped(device, meta_ref)[:2]
        starts = [jnp.maximum(c, 0) for c in chosen]
        lanes = group * sub
        first_key = lax.broadcasted_iota(jnp.int32, (2 * rows, 2 * lanes), 0) < rows
        first_row = lax.broadcasted_iota(jnp.int32, (2 * rows, 2 * lanes), 1) < lanes
        bias = jnp.where(first_key == first_row, 0.0, jnp.where(chosen[0] == chosen[1], 0.0, NEG))
        names = [range(g * group, (g + 1) * group) for g in range(kv_heads)]
        cols = [slice(g * HD, (g + 1) * HD) for g in range(kv_heads)]
        finals, logs = update(
            [
                jnp.concatenate([sub_ref[pl.ds(c * kv_heads + g, 1), :] for c in starts], axis=1)
                for g in range(kv_heads)
            ],
            [rows_of(base_ref, starts, n) for n in names],
            [kv[0, :, c] for c in cols],
            [kv[1, :, c] for c in cols],
            [rows_of(q_ref, starts, n) for n in names],
            bias,
        )
        for slot in range(2):
            at_rows = pl.ds(pl.multiple_of(starts[slot] * sub, sub), sub)
            for g in range(kv_heads):
                new_ref[slot * kv_heads + g : slot * kv_heads + g + 1, :] = logs[g][:, slot * lanes : (slot + 1) * lanes]

            @pl.when(chosen[slot] >= 0)
            def _():
                for g in range(kv_heads):
                    for i, j in enumerate(names[g]):
                        at = slot * lanes + i * sub
                        full_ref[at_rows, j * HD : (j + 1) * HD] = finals[g][at : at + sub]

    half_rows = rows // 2
    mine_ref[...] = full_ref[pl.ds(pl.multiple_of(head * half_rows, half_rows), half_rows), :]
    first = (1 - last_sent(device, head, meta_ref)) * sub + (1 - head) * half_rows
    send_ref[...] = full_ref[pl.ds(pl.multiple_of(first, sub), sub), :]


def late_kernel(half, idx_ref, meta_ref, q_ref, full_ref, table_ref, new_ref, h, late_ref, send_ref, log_ref):
    rows = q_ref.shape[0]
    sub = rows // QB
    kv_heads = h.shape[2] // HD
    group = q_ref.shape[1] // h.shape[2]
    device = idx_ref[0]
    head = idx_ref[1]
    first, second, chosen = helped(device, meta_ref)
    at_send = last_sent(device, head, meta_ref) * sub + (1 - head) * (rows // 2)
    send_ref[...] = full_ref[pl.ds(pl.multiple_of(at_send, sub), sub), :]

    @pl.when(chosen >= 0)
    def _():
        names = [range(g * group, (g + 1) * group) for g in range(kv_heads)]
        cols = [slice(g * HD, (g + 1) * HD) for g in range(kv_heads)]
        old_logs = []
        for g in range(kv_heads):
            old_log = table_ref[pl.ds(chosen * kv_heads + g, 1), :]
            old_log = jnp.where(first == chosen, new_ref[g : g + 1, :], old_log)
            old_logs.append(jnp.where(second == chosen, new_ref[kv_heads + g : kv_heads + g + 1, :], old_log))
        finals, logs = update(
            old_logs,
            [rows_of(full_ref, [chosen], n) for n in names],
            [h[0, :, c] for c in cols],
            [h[1, :, c] for c in cols],
            [rows_of(q_ref, [chosen], n) for n in names],
            None,
        )
        for g in range(kv_heads):
            log_ref[g : g + 1, :] = logs[g]
        here = chosen // (QB // 2) == head

        @pl.when(here)
        def _():
            for g in range(kv_heads):
                for i, j in enumerate(names[g]):
                    late_ref[:, j * HD : (j + 1) * HD] = finals[g][i * sub : (i + 1) * sub]

        @pl.when(jnp.logical_not(here))
        def _():
            for g in range(kv_heads):
                for i, j in enumerate(names[g]):
                    send_ref[:, j * HD : (j + 1) * HD] = finals[g][i * sub : (i + 1) * sub]


def log_kernel(idx_ref, meta_ref, old_ref, new_ref, late_ref, log_ref):
    heads, rows = log_ref.shape
    kv_heads = late_ref.shape[0]
    group = heads // kv_heads
    sub = rows // QB
    row_sub = lax.broadcasted_iota(jnp.int32, (1, rows), 1) // sub
    results = [old_ref[j : j + 1, :] for j in range(heads)]
    sources = (new_ref[:kv_heads, :], new_ref[kv_heads:, :], late_ref[...])
    for chosen, source in zip(helped(idx_ref[0], meta_ref), sources):
        for i in range(group):
            moved = pltpu.roll(source, (chosen + QB - i) % QB * sub, 1)
            for g in range(kv_heads):
                j = g * group + i
                results[j] = jnp.where(row_sub == chosen, moved[g : g + 1, :], results[j])
    for j in range(heads):
        log_ref[j : j + 1, :] = results[j] * LN2


def call(kernel, name, outs, scratch, *args, scalars):
    return pl.pallas_call(
        kernel,
        out_shape=outs,
        in_specs=[SMEM] * scalars + [VMEM] * (len(args) - scalars),
        out_specs=[SMEM if out.shape == (STEPS,) else VMEM for out in outs],
        scratch_shapes=scratch,
        compiler_params=PARAMS,
        cost_estimate=COST,
        name=name,
    )(*args)


def shards(query, key, value, held_kv, plan):
    rows = query.shape[0]
    sub = rows // QB
    wide = query.shape[1]
    kv_heads = key.shape[1] // HD
    group = wide // key.shape[1]
    size = lax.axis_size("ctx")
    half = size // 2
    device = lax.axis_index("ctx")
    head = lax.axis_index("head")
    idx = jnp.stack([device, head]).astype(jnp.int32)

    def send(x, route):
        return lax.ppermute(x, "ctx", route)

    def other_head(x):
        return lax.ppermute(x, "head", [(0, 1), (1, 0)])

    def f32(*shape):
        return jax.ShapeDtypeStruct(shape, jnp.float32)

    def b16(*shape):
        return jax.ShapeDtypeStruct(shape, jnp.bfloat16)

    swap = [(i, i ^ 1) for i in range(size)]
    two_on = swap[: half - 2] + [(i, i + 2) for i in range(half - 2, size - 2)]
    two_on += [(i, i - half) for i in range(size - 2, size)]
    across = [(i, i + half + 1) for i in range(half - 2)] + swap[half - 2 : half]
    across += [(i, i - half) for i in range(half, size - 2)] + [(size - 2, size - 1), (size - 1, half)]
    extra = [(half - 2, size - 1), (size - 1, size - 2), (size - 2, half - 1), (half - 1, half - 2)]
    moved = {i for i, _ in extra}
    extra += [(i, j) for i, j in swap if i not in moved]
    beside = swap[:half] + [(i, half + (i - half + (1 if i % 2 else -1)) % half) for i in range(half, size)]

    n2 = send(held_kv, two_on)
    sx = send(held_kv, swap)
    f = send(held_kv, across)
    acc, stat, meta = call(
        functools.partial(local_kernel, half, plan.shape[0]),
        "local",
        (f32(kv_heads, HD, group * rows), f32(kv_heads, 2, group * rows), jax.ShapeDtypeStruct((STEPS,), jnp.int32)),
        (),
        idx, plan, query, key, value, held_kv,
        scalars=2,
    )
    held_late, acc = lax.optimization_barrier((held_kv, acc))
    g1 = send(held_late, extra)
    pair = pltpu.VMEM((2, 2 * rows, key.shape[1]), jnp.bfloat16)
    outs = (b16(rows, wide), f32(kv_heads * group, rows), f32(QB * kv_heads, group * sub))
    state = (f32(kv_heads, HD, group * rows), f32(kv_heads, 2, group * rows))
    held_late, acc = lax.optimization_barrier((held_kv, acc))
    g1 = send(held_late, extra)
    chosen = jnp.where(device % 2 == 0, meta[2], meta[0]) - head * (QB // 2)
    row_sub = lax.broadcasted_iota(jnp.int32, (rows // 2, 1), 0) // sub
    last = jnp.where((chosen >= 0) & (chosen < QB // 2), chosen, 1)
    n2, acc, chosen, last = lax.optimization_barrier((n2, acc, chosen, last))

    def two_back(n2, acc, stat):
        sn2 = send(n2, swap)
        args = (idx, query, acc, stat, n2)
        return [sn2, *call(functools.partial(two_back_kernel, half), "two_back", state, (), *args, scalars=1)]

    def none(n2, acc, stat):
        return [n2, acc, stat]

    sn2, acc, stat = lax.cond(plan[0, 0] >= 0, two_back, none, n2, acc, stat)
    f, acc = lax.optimization_barrier((f, acc))
    h = send(f, beside)
    sf = send(f, swap)
    sg = send(g1, swap)
    one = pltpu.VMEM(held_kv.shape, jnp.bfloat16)
    base, logs, table = call(
        functools.partial(near_kernel, half), "near", outs, (one,), idx, query, acc, stat, sx, sn2, scalars=1
    )
    full, mine, away, new = call(
        functools.partial(early_kernel, half),
        "early",
        (b16(rows, wide), b16(rows // 2, wide), b16(sub, wide), f32(2 * kv_heads, group * sub)),
        (pair,),
        idx, meta, query, base, table, f, sf, g1, sg,
        scalars=2,
    )
    there = other_head(away)
    h, full = lax.optimization_barrier((h, full))
    late, late_away, late_log = call(
        functools.partial(late_kernel, half),
        "late",
        (b16(sub, wide), b16(sub, wide), f32(kv_heads, group * sub)),
        (),
        idx, meta, query, full, table, new, h,
        scalars=2,
    )
    late_there = other_head(late_away)
    new, there = lax.optimization_barrier((new, there))
    (log_total,) = call(
        log_kernel, "logs", (f32(kv_heads * group, rows),), (), idx, meta, logs, new, late_log, scalars=2
    )
    mine = jnp.where(row_sub == chosen, jnp.concatenate([late] * (QB // 2), axis=0), mine)
    there = jnp.where(
        row_sub == last,
        jnp.concatenate([late_there] * (QB // 2), axis=0),
        jnp.concatenate([there] * (QB // 2), axis=0),
    )
    attended = jnp.where(
        head == 0,
        jnp.concatenate([mine, there], axis=1),
        jnp.concatenate([there, mine], axis=1),
    )
    return (attended, log_total)


def solution(mesh):
    return jax.shard_map(
        shards,
        mesh=mesh,
        in_specs=(
            P("ctx", "head"),
            P("ctx", "head"),
            P("ctx", "head"),
            P(None, "ctx", "head"),
            P(),
        ),
        out_specs=(P(("ctx", "head"), None), P("head", "ctx")),
        check_vma=False,
    )
```
